32 devices in a mesh: groups: 2 (over y), side: 8 (over z, x), tp: 2 (over core).
Axes of the slice: x: 2, y: 2, z: 4, core: 2. Of those that a mesh axis runs over, the one named last changes fastest.
Arguments:
- residual: bfloat16 [2, 32, 3072], P(None, ('groups', 'side'), 'tp'), parts along dimension 1, may hold values from -5 to 5
- queries: bfloat16 [2, 32, 3072], P(None, ('groups', 'side'), 'tp'), parts along dimension 1, may hold values from -24 to 24
- key_cache: bfloat16 [128, 16, 512], P(('groups', 'side'), None, 'tp'), parts along dimension 0, may hold values from -6 to 6
- value_cache: bfloat16 [128, 16, 512], P(('groups', 'side'), None, 'tp'), parts along dimension 0, may hold values from -6 to 6
- page_table: int32 [2, 32, 2], P(None, ('groups', 'side')), parts along dimension 1, may hold values from 0 to 7, as said below
- lengths: int32 [2, 32], P(None, ('groups', 'side')), parts along dimension 1, may hold values from 2 to 32, as said below
- routes: int32 [2, 32, 2], P(None, ('groups', 'side')), parts along dimension 1, may hold values from 0 to 3, all different within a row; in each aligned block of 2 rows (0 to 1, 2 to 3, ..., all dimensions but the last counted through in order) at most 2 rows name the same one
- gate_fixed: int32 [2, 32], P(None, ('groups', 'side')), parts along dimension 1, may hold values from 6554 to 58981
- norm_gain: bfloat16 [3072], replicated, may hold values from 0.099609375 to 1.8984375
- w_gate: bfloat16 [3072, 65536], P(None, ('side', 'tp')), may hold values from -0.109375 to 0.109375
- w_up: bfloat16 [3072, 65536], P(None, ('side', 'tp')), may hold values from -0.109375 to 0.109375
- w_down: bfloat16 [65536, 3072], P('side', 'tp'), may hold values from -0.046875 to 0.046875
Outputs:
- layer_out: bfloat16 [2, 32, 3072], P(None, ('groups', 'side'), 'tp'), parts along dimension 1
The draws below stay inside these ranges and needn't reach their ends.
There are 2 independent parts, one for each index of `groups`. The reference program is written for one: setup_inputs(seed, part) draws one part's arguments, and reference() takes and returns one part's arrays. A program takes and returns all parts, laid end to end along the dimension named above; an argument that names none is the same for every part. Nothing has to cross between parts.
Inputs may be any that keep to these rules, and one draw needn't show every extreme that they name: `page_table`: on each index of side, the 2 x 2 x 2 entries of its requests are a permutation of its 8 pages. `lengths`: positions of a request's cache, its current token included; some request holds 32. `routes`: each token names two different experts; among the 2 tokens of one micro-batch on one index of side, no expert is named more than 2 times.
All inputs are finite; a program needn't handle non-finite values.
Results may differ from the reference program's by a relative error of at most 0.0075.
Values may be sent and summed in bfloat16 or wider, within the bound.
No kernel may reach another device: no remote copies, remote signals or barrier semaphores. Data moves between devices by JAX's collectives and lax.ppermute only.
A program may use at most 192 MiB of HBM per device.

```python
import math
import jax
import jax.numpy as jnp
import numpy as np
from jax import lax

D = 3072
HEADS = 24
KV_HEADS = 4
HEAD_DIM = 128
EXPERTS = 4
FF = 16384
TOPK = 2
MB = 2
TOK_DEV = 2
PAGE = 16
MAXP = 2
CAP = 2
MAXLEN = 32
PAGES_DEV = 8
TOKENS = 16
PAGES = 64


def page_layout(key):
    devices = TOKENS // TOK_DEV
    subkeys = jax.random.split(jax.random.fold_in(key, 103), devices)
    orders = jax.vmap(lambda single: jax.random.permutation(single, PAGES_DEV))(subkeys)
    orders = orders.reshape(devices, MB, TOK_DEV, MAXP).transpose(1, 0, 2, 3)
    return orders.reshape(MB, TOKENS, MAXP).astype(jnp.int32)


def draw_page_table(key, part):
    return page_layout(key)


def draw_lengths(key, part):
    key = jax.random.fold_in(key, 4)
    sub_a, sub_b = jax.random.split(key)
    devices = TOKENS // TOK_DEV
    device_cap = jax.random.randint(sub_a, (1, devices, 1), MAXLEN // 4, MAXLEN + 1)
    raw_draw = jax.random.randint(sub_b, (MB, devices, TOK_DEV), 0, MAXLEN)
    counted = 2 + raw_draw % (device_cap - 1)
    counted = counted.reshape(MB, TOKENS).at[0, 0].set(MAXLEN)
    return counted.astype(jnp.int32)


def draw_residual(key, part):
    key = jax.random.fold_in(key, 5)
    sub_a, sub_b, sub_c = jax.random.split(key, 3)
    col_scale = jnp.exp(jax.random.uniform(sub_a, (1, 1, D), minval=math.log(0.2), maxval=math.log(2.0)))
    row_scale = jnp.exp(jax.random.uniform(sub_b, (MB, TOKENS, 1), minval=math.log(0.5), maxval=math.log(1.0)))
    normals = jnp.clip(jax.random.normal(sub_c, (MB, TOKENS, D)), -2.5, 2.5)
    return (normals * col_scale * row_scale).astype(jnp.bfloat16)


def draw_key_cache(key, part):
    key = jax.random.fold_in(key, 7)
    normals = jnp.clip(jax.random.normal(key, (PAGES, PAGE, KV_HEADS * HEAD_DIM)), -6.0, 6.0)
    return normals.astype(jnp.bfloat16)


def draw_queries(key, part):
    key = jax.random.fold_in(key, 9)
    normals = jnp.clip(jax.random.normal(key, (MB, TOKENS, HEADS * HEAD_DIM)), -6.0, 6.0)
    return normals.astype(jnp.bfloat16)


def with_ends(drawn, rng, low, high):
    shape = drawn.shape
    spot = [jax.random.randint(jax.random.fold_in(rng, axis), (), 0, shape[axis]) for axis in range(len(shape))]
    drawn = drawn.at[tuple(spot)].set(low)
    longest = shape.index(max(shape))
    spot[longest] = (spot[longest] + 1) % shape[longest]
    return drawn.at[tuple(spot)].set(high)


def levels(rng, dims, cuts, low, high):
    gain = 1.0
    for dim, parts in cuts:
        steps = jax.random.uniform(jax.random.fold_in(jax.random.fold_in(rng, 6), dim), (parts,), jnp.float32, low / len(cuts), high / len(cuts))
        gain = gain * jnp.repeat(jnp.exp(steps), dims[dim] // parts).reshape((-1,) + (1,) * (len(dims) - 1 - dim))
    return gain


def deal_out(stream_key, own, number, rows, number_of, top, reach, lean):
    order = jax.random.permutation(stream_key, number_of)
    packed, ordinary = shares(number_of, rows * top, reach, lean, True), shares(number_of, rows * top, reach, lean, False)
    places = jnp.arange(number_of)

    def named(sizes, turn):
        used = int((sizes > 0).sum())
        fixed = max(1, used // 4)
        passed = fixed + (places - fixed + turn * (used - fixed)) % max(1, number_of - fixed)
        return jnp.zeros((number_of,), jnp.int32).at[order[jnp.where(places < fixed, places, passed)]].set(jnp.asarray(sizes, jnp.int32))

    sizes = jnp.where(number % 4 == 0, named(packed, number // 4), named(ordinary, number - number // 4 - 1))
    mixed = jax.random.permutation(jax.random.fold_in(own, 3), number_of)
    source_of, taker = mixed[0:number_of // 2 * 2:2], mixed[1:number_of // 2 * 2:2]
    margin = jnp.minimum(sizes[source_of] - 1, reach - sizes[taker]) // 2
    margin = jnp.where((source_of == order[0]) | (taker == order[0]) | (sizes[taker] == 0), 0, jnp.maximum(margin, 0))
    passed = jax.random.randint(jax.random.fold_in(own, 4), (number_of // 2,), 0, 1 << 20) % (margin + 1)
    sizes = sizes.at[source_of].add(-passed).at[taker].add(passed)
    items = jnp.searchsorted(jnp.cumsum(sizes), jnp.arange(rows * top), side="right").astype(jnp.int32)
    listing = items.reshape(top, rows).T
    listing = listing[jax.random.permutation(jax.random.fold_in(own, 1), rows)]
    turn = jax.random.randint(jax.random.fold_in(own, 2), (rows, 1), 0, top)
    return jnp.take_along_axis(listing, (jnp.arange(top)[None, :] + turn) % top, axis=1)


def shares(count, total, limit, skew, full):
    loads = [(1 << 20) // math.isqrt(rank ** skew) + 1 for rank in range(1, count + 1)]
    largest = limit if full else min(limit, max(-(-total // count), total * loads[0] // sum(loads)))
    least = 1 if total - largest >= count - 1 else 0
    counts, rest = [largest] + [least] * (count - 1), total - largest - least * (count - 1)
    while rest > 0:
        candidates = [i for i in range(1, count) if counts[i] < largest] or [i for i in range(1, count) if counts[i] < limit]
        pool, left = sum([loads[i] for i in candidates]), rest
        for i in candidates:
            more = min(limit - counts[i], max(1, left * loads[i] // pool), rest)
            counts[i] = counts[i] + more
            rest = rest - more
    return np.array(counts)


def gaussian(stream_key, dims, spread, bound, cuts=(), kind=jnp.bfloat16):
    values = jax.random.normal(stream_key, dims, jnp.float32) * spread
    if len(cuts) > 0:
        values = levels(stream_key, dims, cuts, -0.22, 0.18) * values
    return jnp.clip(values, min=-bound, max=bound).astype(kind)


def setup_inputs(seed: int = 0, part: int = 0) -> dict:
    splits = jax.random.split(jax.random.key(seed), 13)
    part_splits = jax.random.split(jax.random.fold_in(splits[12], part), 13)
    residual = draw_residual(jax.random.fold_in(jax.random.fold_in(splits[12], part), 71), part)
    queries = draw_queries(jax.random.fold_in(jax.random.fold_in(splits[12], part), 71), part)
    key_cache = draw_key_cache(jax.random.fold_in(jax.random.fold_in(splits[12], part), 71), part)
    value_cache = gaussian(part_splits[3], (PAGES, PAGE, KV_HEADS * HEAD_DIM), 1.0, 6.0, ((0, 8), (2, 2)))
    page_table = draw_page_table(jax.random.fold_in(jax.random.fold_in(splits[12], part), 71), part)
    lengths = draw_lengths(jax.random.fold_in(jax.random.fold_in(splits[12], part), 71), part)
    routes_keys = jax.random.split(jax.random.fold_in(part_splits[6], 1), MB * TOKENS // TOK_DEV)
    routes_turns = jax.random.permutation(jax.random.fold_in(part_splits[6], 3), MB * TOKENS // TOK_DEV)
    routes = jax.vmap(lambda own, number: deal_out(jax.random.fold_in(part_splits[6], 2), own, number, TOK_DEV, EXPERTS, TOPK, CAP, 1))(routes_keys, routes_turns).reshape((MB, TOKENS, TOPK))
    gate_fixed = with_ends(jax.random.randint(part_splits[7], (MB, TOKENS), 6554, 58982), jax.random.fold_in(part_splits[7], 1), 6554, 58981).astype(jnp.int32)
    norm_gain = jnp.clip(1.0 + 0.18 * jax.random.normal(splits[8], (D,), jnp.float32), 0.099609375, 1.8984375).astype(jnp.bfloat16)
    w_gate = gaussian(splits[9], (D, EXPERTS * FF), D ** -0.5, 0.109375, ((1, 16),))
    w_up = gaussian(splits[10], (D, EXPERTS * FF), D ** -0.5, 0.109375, ((1, 16),))
    w_down = gaussian(splits[11], (EXPERTS * FF, D), FF ** -0.5, 0.046875, ((0, 8), (1, 2)))
    return {"residual": residual, "queries": queries, "key_cache": key_cache, "value_cache": value_cache, "page_table": page_table, "lengths": lengths, "routes": routes, "gate_fixed": gate_fixed, "norm_gain": norm_gain, "w_gate": w_gate, "w_up": w_up, "w_down": w_down}


EPS = 1e-05
GATE_ONE = 65536.0

def attend_token(query_row, key_rows, value_rows, length):
    per_group = HEADS // KV_HEADS
    inv_root = 1.0 / math.sqrt(HEAD_DIM)
    key_heads = key_rows.reshape(MAXLEN, KV_HEADS, HEAD_DIM).astype(jnp.float32)
    value_heads = value_rows.reshape(MAXLEN, KV_HEADS, HEAD_DIM).astype(jnp.float32)
    query_heads = query_row.reshape(KV_HEADS, per_group, HEAD_DIM).astype(jnp.float32)
    scores = jnp.einsum('kgd,lkd->kgl', query_heads, key_heads, precision=lax.Precision.HIGHEST) * inv_root
    is_live = jnp.arange(MAXLEN, dtype=jnp.int32) < length
    scores = jnp.where(is_live, scores, -1e+30)
    row_max = lax.optimization_barrier(jnp.max(scores, axis=-1, keepdims=True))
    unnorm = jnp.where(is_live, jnp.exp(scores - row_max), 0.0)
    denom_sum = lax.optimization_barrier(jnp.sum(unnorm, axis=-1, keepdims=True))
    probs = lax.optimization_barrier(unnorm.astype(jnp.bfloat16)).astype(jnp.float32)
    blended = jnp.einsum('kgl,lkd->kgd', probs, value_heads, precision=lax.Precision.HIGHEST) / denom_sum
    return blended.reshape(-1)

def reference(residual, queries, key_cache, value_cache, page_table, lengths, routes, gate_fixed, norm_gain, w_gate, w_up, w_down):
    device = jnp.arange(TOKENS, dtype=jnp.int32) // TOK_DEV
    gain_full = norm_gain.astype(jnp.float32)
    results = []
    for micro_idx in range(MB):
        page_ids = page_table[micro_idx] + (device * PAGES_DEV)[:, None]

        def single(packed_args):
            query_row, pages_row, length = packed_args
            key_rows = key_cache[pages_row].reshape(MAXLEN, KV_HEADS * HEAD_DIM)
            value_rows = value_cache[pages_row].reshape(MAXLEN, KV_HEADS * HEAD_DIM)
            return attend_token(query_row, key_rows, value_rows, length)
        attended = lax.map(single, (queries[micro_idx], page_ids, lengths[micro_idx]))
        carried = (residual[micro_idx].astype(jnp.float32) + attended).astype(jnp.bfloat16)
        whole_rows = lax.optimization_barrier(carried).astype(jnp.float32)
        inv_rms = lax.rsqrt(lax.optimization_barrier(jnp.mean(whole_rows * whole_rows, axis=-1, keepdims=True)) + EPS)
        normed = (whole_rows * inv_rms * gain_full).astype(jnp.bfloat16)
        expert_ids = routes[micro_idx]
        first_gate = gate_fixed[micro_idx].astype(jnp.float32) / GATE_ONE
        second = (GATE_ONE - gate_fixed[micro_idx].astype(jnp.float32)) / GATE_ONE
        moe_sum = jnp.zeros((TOKENS, D), jnp.float32)
        for expert in range(EXPERTS):
            start = expert * FF
            gate_proj = jnp.dot(normed, w_gate[:, start:start + FF], preferred_element_type=jnp.float32)
            up_proj = jnp.dot(normed, w_up[:, start:start + FF], preferred_element_type=jnp.float32)
            hidden = (jax.nn.silu(gate_proj) * up_proj).astype(jnp.bfloat16)
            result = jnp.dot(hidden, w_down[start:start + FF], preferred_element_type=jnp.float32)
            weight = jnp.where(expert_ids[:, 0] == expert, first_gate, 0.0) + jnp.where(expert_ids[:, 1] == expert, second, 0.0)
            moe_sum = moe_sum + weight[:, None] * result
        results.append((whole_rows + moe_sum).astype(jnp.bfloat16))
    return jnp.stack(results)
```

```python
import functools
import math

import jax
import jax.numpy as jnp
from jax import lax
from jax.experimental import pallas as pl
from jax.experimental.pallas import tpu as pltpu
from jax.sharding import PartitionSpec as P

HEAD_DIM = 128
EXPERTS = 4
EPS = 1e-05
GATE_ONE = 65536.0
LANES = 128
SMALL = 2 << 20


def by_row(shape, scalars):
    token = lax.broadcasted_iota(jnp.int32, shape, 0) % len(scalars)
    out = jnp.full(shape, scalars[0])
    for idx in range(1, len(scalars)):
        out = jnp.where(token == idx, scalars[idx], out)
    return out


def flat(ref):
    return jnp.concatenate([ref[idx].astype(jnp.float32) for idx in range(ref.shape[0])], axis=0)


def attend_kernel(where_ref, pages_ref, len_ref, routes_ref, gate_ref, res_ref, q_ref, k_ref, v_ref, _w0_ref, _w1_ref, out_ref):
    micro, dev, half = res_ref.shape
    tok = micro * dev
    pages, page, kv_width = k_ref.shape
    kv_local = kv_width // HEAD_DIM
    group = half // kv_width
    inv_root = 1.0 / math.sqrt(HEAD_DIM)
    keys = k_ref[...].reshape(pages * page, kv_width)
    values = v_ref[...].reshape(pages * page, kv_width)
    shape = (group * tok, pages * page)
    slot = lax.broadcasted_iota(jnp.int32, shape, 1)
    slot_page, offset = slot // page, slot % page
    position = jnp.full(shape, 1 << 20, jnp.int32)
    for nth in range(pages_ref.shape[2]):
        owner = by_row(shape, [pages_ref[t // dev, t % dev, nth] for t in range(tok)])
        position = jnp.where(slot_page == owner, offset + nth * page, position)
    live = position < by_row(shape, [len_ref[t // dev, t % dev] for t in range(tok)])
    queries = flat(q_ref)
    residual = flat(res_ref)
    for head in range(kv_local):
        cols = slice(head * HEAD_DIM, (head + 1) * HEAD_DIM)
        first = head * group
        rows = jnp.concatenate(
            [
                queries[:, (first + g) * HEAD_DIM : (first + g + 1) * HEAD_DIM]
                for g in range(group)
            ],
            axis=0,
        ).astype(jnp.bfloat16)
        scores = lax.dot_general(
            rows, keys[:, cols], (((1,), (1,)), ((), ())), preferred_element_type=jnp.float32
        )
        scores = jnp.where(live, scores * inv_root, -1e30)
        row_max = jnp.max(scores, axis=-1, keepdims=True)
        unnorm = jnp.where(live, jnp.exp(scores - row_max), 0.0)
        denom = jnp.sum(unnorm, axis=-1, keepdims=True)
        blended = (
            jnp.dot(
                unnorm.astype(jnp.bfloat16), values[:, cols], preferred_element_type=jnp.float32
            )
            / denom
        )
        for g in range(group):
            at = slice((first + g) * HEAD_DIM, (first + g + 1) * HEAD_DIM)
            carried = residual[:, at] + blended[g * tok : (g + 1) * tok]
            out_ref[:, at] = carried.astype(jnp.bfloat16)
    lane = lax.broadcasted_iota(jnp.int32, (tok, LANES), 1)
    expert = lane % EXPERTS
    fixed = by_row((tok, LANES), [gate_ref[t // dev, t % dev] for t in range(tok)])
    one = by_row((tok, LANES), [routes_ref[t // dev, t % dev, 0] for t in range(tok)])
    two = by_row((tok, LANES), [routes_ref[t // dev, t % dev, 1] for t in range(tok)])
    fixed = fixed.astype(jnp.float32)
    weight = jnp.where(expert == one, fixed / GATE_ONE, 0.0) + jnp.where(
        expert == two, (GATE_ONE - fixed) / GATE_ONE, 0.0
    )
    high = weight.astype(jnp.bfloat16).astype(jnp.float32)
    mid = (weight - high).astype(jnp.bfloat16).astype(jnp.float32)
    low = weight - high - mid
    term = lane // EXPERTS
    packed = jnp.where(
        term == 0, high, jnp.where(term == 1, mid, jnp.where(term == 2, low, 0.0))
    )
    out_ref[:, half:] = packed.astype(jnp.bfloat16)


def join_kernel(one_ref, two_ref, out_ref):
    out_ref[...] = jnp.concatenate([one_ref[...], two_ref[...]], axis=0)


def fetch(w_ref, buf_ref, sem, start):
    chunks, depth, _ = buf_ref.shape
    copies = []
    for idx in range(chunks):
        copies.append(
            pltpu.make_async_copy(
                w_ref.at[pl.ds(pl.multiple_of(start + idx * depth, depth), depth), :],
                buf_ref.at[idx],
                sem.at[idx],
            )
        )
        copies[-1].start()
    return copies


def hidden_kernel(
    where_ref, own_ref, other_ref, gain_ref, wg_ref, wu_ref, out_ref, x_ref, gate_ref, buf_ref, sem
):
    chunks, depth, _ = buf_ref.shape
    half = own_ref.shape[1] - LANES
    copies = fetch(wu_ref, buf_ref, sem, 0)
    is_first = where_ref[0] == 0
    own = own_ref[:, :half].astype(jnp.float32)
    other = other_ref[:, :half].astype(jnp.float32)
    square = jnp.sum(own * own, axis=-1, keepdims=True)
    square = square + jnp.sum(other * other, axis=-1, keepdims=True)
    inv_rms = lax.rsqrt(square / (2 * half) + EPS)
    left = jnp.where(is_first, own, other)
    right = jnp.where(is_first, other, own)
    gain = gain_ref[...].astype(jnp.float32).reshape(1, -1)
    x_ref[:, :half] = (left * inv_rms * gain[:, :half]).astype(jnp.bfloat16)
    x_ref[:, half:] = (right * inv_rms * gain[:, half:]).astype(jnp.bfloat16)
    gate = jnp.dot(x_ref[...], wg_ref[...], preferred_element_type=jnp.float32)
    gate_ref[...] = gate / (1.0 + jnp.exp(-gate))
    up = None
    for idx, copy in enumerate(copies):
        copy.wait()
        part = jnp.dot(
            x_ref[:, idx * depth : (idx + 1) * depth],
            buf_ref[idx],
            preferred_element_type=jnp.float32,
        )
        up = part if up is None else up + part
    out_ref[...] = (gate_ref[...] * up).astype(jnp.bfloat16)


def down_own_kernel(where_ref, hid_ref, w_ref, out_ref, buf_ref, sem):
    chunks, depth, _ = buf_ref.shape
    copies = fetch(w_ref, buf_ref, sem, where_ref[0] * chunks * depth)
    for idx, copy in enumerate(copies):
        copy.wait()
        part = jnp.dot(
            hid_ref[:, idx * depth : (idx + 1) * depth],
            buf_ref[idx],
            preferred_element_type=jnp.float32,
        )
        out_ref[...] = part if idx == 0 else out_ref[...] + part


def down_other_kernel(where_ref, hid_ref, part_ref, extra_ref, w_ref, out_ref, buf_ref, sem):
    chunks, depth, _ = buf_ref.shape
    copies = fetch(w_ref, buf_ref, sem, (1 - where_ref[0]) * chunks * depth)
    total = part_ref[...]
    for idx, copy in enumerate(copies):
        copy.wait()
        total = total + jnp.dot(
            hid_ref[:, idx * depth : (idx + 1) * depth],
            buf_ref[idx],
            preferred_element_type=jnp.float32,
        )
    extra = extra_ref[...].astype(jnp.float32)
    lane = lax.broadcasted_iota(jnp.int32, extra.shape, 1)
    mine = (lane % EXPERTS == where_ref[1]) & (lane < 3 * EXPERTS)
    weight = jnp.sum(jnp.where(mine, extra, 0.0), axis=-1, keepdims=True)
    out_ref[...] = (total * weight).astype(jnp.bfloat16)


SMEM = pl.BlockSpec(memory_space=pltpu.SMEM)
VMEM = pl.BlockSpec(memory_space=pltpu.VMEM)
ANY = pl.BlockSpec(memory_space=pl.ANY)


def call(kernel, out_shape, in_specs, args, scratch=(), limit=SMALL):
    return pl.pallas_call(
        kernel,
        out_shape=out_shape,
        in_specs=in_specs,
        out_specs=jax.tree.map(lambda _: VMEM, out_shape),
        scratch_shapes=scratch,
        compiler_params=pltpu.CompilerParams(vmem_limit_bytes=limit),
    )(*args)


def in_vmem(array):
    return pltpu.with_memory_space_constraint(array, pltpu.VMEM)


def in_hbm(array):
    return pltpu.with_memory_space_constraint(array, pltpu.HBM)


def swap(array, axis, mask):
    size = lax.axis_size(axis)
    return lax.ppermute(array, axis, [(i, i ^ mask) for i in range(size)])


def per_device(
    residual,
    queries,
    key_cache,
    value_cache,
    page_table,
    lengths,
    routes,
    gate_fixed,
    norm_gain,
    w_gate,
    w_up,
    w_down,
):
    micro_count, tok_dev, half = residual.shape
    side_size = lax.axis_size("side")
    tok = micro_count * tok_dev
    rows = tok * side_size
    span = side_size // EXPERTS
    small = SMALL + 64 * rows * half
    width = w_gate.shape[1]
    where = jnp.stack([lax.axis_index("tp"), lax.axis_index("side") // span]).astype(jnp.int32)
    local = call(
        attend_kernel,
        jax.ShapeDtypeStruct((tok, half + LANES), jnp.bfloat16),
        [SMEM] * 5 + [VMEM] * 4 + [ANY] * 2,
        (
            where,
            page_table,
            lengths,
            routes,
            gate_fixed,
            residual,
            queries,
            key_cache,
            value_cache,
            in_hbm(w_gate),
            in_hbm(w_up),
        ),
    )
    gathered = local
    masks = [1 << bit for bit in range(side_size.bit_length() - 1)]
    for mask in masks:
        shape = (2 * gathered.shape[0], gathered.shape[1])
        gathered = call(
            join_kernel,
            jax.ShapeDtypeStruct(shape, gathered.dtype),
            [VMEM] * 2,
            (gathered, swap(gathered, "side", mask)),
            limit=small,
        )
    other = swap(gathered, "tp", 1)
    up_chunks = 6
    hidden = call(
        hidden_kernel,
        jax.ShapeDtypeStruct((rows, width), jnp.bfloat16),
        [SMEM] + [VMEM] * 4 + [ANY],
        (where, gathered, other, norm_gain, in_vmem(w_gate), in_hbm(w_up)),
        (
            pltpu.VMEM((rows, 2 * half), jnp.bfloat16),
            pltpu.VMEM((rows, width), jnp.float32),
            pltpu.VMEM((up_chunks, 2 * half // up_chunks, width), jnp.bfloat16),
            pltpu.SemaphoreType.DMA((up_chunks,)),
        ),
        small + w_up.size * w_up.dtype.itemsize,
    )
    hidden_other = swap(hidden, "tp", 1)
    chunks = max(1, width // 1024)
    stream = (
        pltpu.VMEM((chunks, width // chunks, half), jnp.bfloat16),
        pltpu.SemaphoreType.DMA((chunks,)),
    )
    part = call(
        down_own_kernel,
        jax.ShapeDtypeStruct((rows, half), jnp.float32),
        [SMEM, VMEM, ANY],
        (where, hidden, in_hbm(w_down)),
        stream,
        small + w_down.size * w_down.dtype.itemsize // 2,
    )
    sent = call(
        down_other_kernel,
        jax.ShapeDtypeStruct((rows, half), jnp.bfloat16),
        [SMEM] + [VMEM] * 3 + [ANY],
        (where, hidden_other, part, gathered[:, half:], in_hbm(w_down)),
        stream,
        small + w_down.size * w_down.dtype.itemsize // 2,
    )
    for mask in reversed(masks):
        count = sent.shape[0] // 2
        received = swap(sent[count:], "side", mask)
        sent = sent[:count].astype(jnp.float32) + received.astype(jnp.float32)
        if mask > 1:
            sent = sent.astype(jnp.bfloat16)
    carried = local[:, :half].astype(jnp.float32)
    return (carried + sent).astype(jnp.bfloat16).reshape(residual.shape)


def solution(mesh):
    in_specs = (
        P(None, ("groups", "side"), "tp"),
        P(None, ("groups", "side"), "tp"),
        P(("groups", "side"), None, "tp"),
        P(("groups", "side"), None, "tp"),
        P(None, ("groups", "side"), None),
        P(None, ("groups", "side")),
        P(None, ("groups", "side"), None),
        P(None, ("groups", "side")),
        P(),
        P(None, ("side", "tp")),
        P(None, ("side", "tp")),
        P("side", "tp"),
    )
    out_specs = P(None, ("groups", "side"), "tp")
    return jax.shard_map(
        per_device, mesh=mesh, in_specs=in_specs, out_specs=out_specs, check_vma=False
    )
```

```python
import functools
import math

import jax
import jax.numpy as jnp
from jax import lax
from jax.experimental import pallas as pl
from jax.experimental.pallas import tpu as pltpu
from jax.sharding import PartitionSpec as P

HEAD_DIM = 128
EXPERTS = 4
EPS = 1e-05
GATE_ONE = 65536.0
LANES = 128
SMALL = 2 << 20


def by_row(shape, scalars):
    token = lax.broadcasted_iota(jnp.int32, shape, 0) % len(scalars)
    out = jnp.full(shape, scalars[0])
    for idx in range(1, len(scalars)):
        out = jnp.where(token == idx, scalars[idx], out)
    return out


def flat(ref):
    return jnp.concatenate([ref[idx].astype(jnp.float32) for idx in range(ref.shape[0])], axis=0)


def attend_kernel(*refs):
    count = 8
    _where, sources, buffers = refs[0], refs[1 : 1 + count], refs[-1 - count : -1]
    out_ref, sem = refs[-2 - count], refs[-1]
    copies = [
        pltpu.make_async_copy(source, buffer, sem.at[idx])
        for idx, (source, buffer) in enumerate(zip(sources, buffers))
    ]
    for copy in copies:
        copy.start()
    for copy in copies:
        copy.wait()
    pages_ref, len_ref, routes_ref, gate_ref, res_ref, q_ref, k_ref, v_ref = buffers
    micro, dev, half = res_ref.shape
    tok = micro * dev
    pages, page, kv_width = k_ref.shape
    kv_local = kv_width // HEAD_DIM
    group = half // kv_width
    inv_root = 1.0 / math.sqrt(HEAD_DIM)
    keys = k_ref[...].reshape(pages * page, kv_width)
    values = v_ref[...].reshape(pages * page, kv_width)
    shape = (group * tok, pages * page)
    slot = lax.broadcasted_iota(jnp.int32, shape, 1)
    slot_page, offset = slot // page, slot % page
    position = jnp.full(shape, 1 << 20, jnp.int32)
    for nth in range(pages_ref.shape[2]):
        owner = by_row(shape, [pages_ref[t // dev, t % dev, nth] for t in range(tok)])
        position = jnp.where(slot_page == owner, offset + nth * page, position)
    live = position < by_row(shape, [len_ref[t // dev, t % dev] for t in range(tok)])
    queries = flat(q_ref)
    residual = flat(res_ref)
    for head in range(kv_local):
        cols = slice(head * HEAD_DIM, (head + 1) * HEAD_DIM)
        first = head * group
        rows = jnp.concatenate(
            [
                queries[:, (first + g) * HEAD_DIM : (first + g + 1) * HEAD_DIM]
                for g in range(group)
            ],
            axis=0,
        ).astype(jnp.bfloat16)
        scores = lax.dot_general(
            rows, keys[:, cols], (((1,), (1,)), ((), ())), preferred_element_type=jnp.float32
        )
        scores = jnp.where(live, scores * inv_root, -1e30)
        row_max = jnp.max(scores, axis=-1, keepdims=True)
        unnorm = jnp.where(live, jnp.exp(scores - row_max), 0.0)
        denom = jnp.sum(unnorm, axis=-1, keepdims=True)
        blended = (
            jnp.dot(
                unnorm.astype(jnp.bfloat16), values[:, cols], preferred_element_type=jnp.float32
            )
            / denom
        )
        for g in range(group):
            at = slice((first + g) * HEAD_DIM, (first + g + 1) * HEAD_DIM)
            carried = residual[:, at] + blended[g * tok : (g + 1) * tok]
            out_ref[:, at] = carried.astype(jnp.bfloat16)
    lane = lax.broadcasted_iota(jnp.int32, (tok, LANES), 1)
    expert = lane % EXPERTS
    fixed = by_row((tok, LANES), [gate_ref[t // dev, t % dev] for t in range(tok)])
    one = by_row((tok, LANES), [routes_ref[t // dev, t % dev, 0] for t in range(tok)])
    two = by_row((tok, LANES), [routes_ref[t // dev, t % dev, 1] for t in range(tok)])
    fixed = fixed.astype(jnp.float32)
    weight = jnp.where(expert == one, fixed / GATE_ONE, 0.0) + jnp.where(
        expert == two, (GATE_ONE - fixed) / GATE_ONE, 0.0
    )
    high = weight.astype(jnp.bfloat16).astype(jnp.float32)
    mid = (weight - high).astype(jnp.bfloat16).astype(jnp.float32)
    low = weight - high - mid
    term = lane // EXPERTS
    packed = jnp.where(
        term == 0, high, jnp.where(term == 1, mid, jnp.where(term == 2, low, 0.0))
    )
    out_ref[:, half:] = packed.astype(jnp.bfloat16)


def join_kernel(one_ref, two_ref, out_ref):
    out_ref[...] = jnp.concatenate([one_ref[...], two_ref[...]], axis=0)


def half_copy(w_ref, out_ref, which, sem):
    depth = out_ref.shape[0]
    start = pl.multiple_of(which * depth, depth)
    return pltpu.make_async_copy(w_ref.at[pl.ds(start, depth), :], out_ref, sem)


def hidden_kernel(
    where_ref,
    own_ref,
    other_ref,
    gain_ref,
    wg_ref,
    wu_ref,
    wd_ref,
    out_ref,
    down_ref,
    x_ref,
    gate_ref,
    buf_ref,
    sem,
    down_sem,
):
    slots, depth, _ = buf_ref.shape
    half = own_ref.shape[1] - LANES
    chunks = 2 * half // depth
    copies = [
        pltpu.make_async_copy(
            wu_ref.at[pl.ds(idx * depth, depth), :], buf_ref.at[idx % slots], sem.at[idx % slots]
        )
        for idx in range(chunks)
    ]
    for copy in copies[:slots]:
        copy.start()
    down = half_copy(wd_ref, down_ref, where_ref[0], down_sem)
    is_first = where_ref[0] == 0
    own = own_ref[:, :half].astype(jnp.float32)
    other = other_ref[:, :half].astype(jnp.float32)
    square = jnp.sum(own * own, axis=-1, keepdims=True)
    square = square + jnp.sum(other * other, axis=-1, keepdims=True)
    inv_rms = lax.rsqrt(square / (2 * half) + EPS)
    left = jnp.where(is_first, own, other)
    right = jnp.where(is_first, other, own)
    gain = gain_ref[...].astype(jnp.float32).reshape(1, -1)
    x_ref[:, :half] = (left * inv_rms * gain[:, :half]).astype(jnp.bfloat16)
    x_ref[:, half:] = (right * inv_rms * gain[:, half:]).astype(jnp.bfloat16)
    gate = jnp.dot(x_ref[...], wg_ref[...], preferred_element_type=jnp.float32)
    gate_ref[...] = gate / (1.0 + jnp.exp(-gate))
    up = None
    for idx, copy in enumerate(copies):
        copy.wait()
        part = jnp.dot(
            x_ref[:, idx * depth : (idx + 1) * depth],
            buf_ref[idx % slots],
            preferred_element_type=jnp.float32,
        )
        if idx + slots < chunks:
            copies[idx + slots].start()
        if idx + slots == chunks:
            down.start()
        up = part if up is None else up + part
    out_ref[...] = (gate_ref[...] * up).astype(jnp.bfloat16)
    down.wait()


def down_own_kernel(where_ref, hid_ref, own_ref, w_ref, out_ref, other_ref, sem):
    copy = half_copy(w_ref, other_ref, 1 - where_ref[0], sem)
    copy.start()
    out_ref[...] = jnp.dot(hid_ref[...], own_ref[...], preferred_element_type=jnp.float32)
    copy.wait()


def down_other_kernel(where_ref, hid_ref, part_ref, extra_ref, w_ref, out_ref):
    total = part_ref[...] + jnp.dot(
        hid_ref[...], w_ref[...], preferred_element_type=jnp.float32
    )
    extra = extra_ref[:, -LANES:].astype(jnp.float32)
    lane = lax.broadcasted_iota(jnp.int32, extra.shape, 1)
    mine = (lane % EXPERTS == where_ref[1]) & (lane < 3 * EXPERTS)
    weight = jnp.sum(jnp.where(mine, extra, 0.0), axis=-1, keepdims=True)
    out_ref[...] = (total * weight).astype(jnp.bfloat16)


def final_kernel(carried_ref, mine_ref, received_ref, out_ref):
    micro, dev, half = out_ref.shape
    total = carried_ref[:, :half].astype(jnp.float32)
    total = total + (
        mine_ref[: micro * dev].astype(jnp.float32) + received_ref[...].astype(jnp.float32)
    )
    for idx in range(micro):
        out_ref[idx] = total[idx * dev : (idx + 1) * dev].astype(jnp.bfloat16)


SMEM = pl.BlockSpec(memory_space=pltpu.SMEM)
VMEM = pl.BlockSpec(memory_space=pltpu.VMEM)
ANY = pl.BlockSpec(memory_space=pl.ANY)


def call(kernel, out_shape, in_specs, args, scratch=(), limit=SMALL):
    return pl.pallas_call(
        kernel,
        out_shape=out_shape,
        in_specs=in_specs,
        out_specs=[VMEM] * len(out_shape) if isinstance(out_shape, tuple) else VMEM,
        scratch_shapes=scratch,
        compiler_params=pltpu.CompilerParams(vmem_limit_bytes=limit),
    )(*args)


def in_vmem(array):
    return pltpu.with_memory_space_constraint(array, pltpu.VMEM)


def in_hbm(array):
    return pltpu.with_memory_space_constraint(array, pltpu.HBM)


def swap(array, axis, mask):
    size = lax.axis_size(axis)
    return lax.ppermute(array, axis, [(i, i ^ mask) for i in range(size)])


def per_device(
    residual,
    queries,
    key_cache,
    value_cache,
    page_table,
    lengths,
    routes,
    gate_fixed,
    norm_gain,
    w_gate,
    w_up,
    w_down,
):
    micro_count, tok_dev, half = residual.shape
    side_size = lax.axis_size("side")
    tok = micro_count * tok_dev
    rows = tok * side_size
    span = side_size // EXPERTS
    small = SMALL + 64 * rows * half
    width = w_gate.shape[1]
    where = jnp.stack([lax.axis_index("tp"), lax.axis_index("side") // span]).astype(jnp.int32)
    small_args = (page_table, lengths, routes, gate_fixed)
    large_args = (residual, queries, key_cache, value_cache)
    local = call(
        attend_kernel,
        jax.ShapeDtypeStruct((tok, half + LANES), jnp.bfloat16),
        [SMEM] + [ANY] * 10,
        (where, *[in_hbm(arg) for arg in (*small_args, *large_args, w_gate, w_up)]),
        (
            *[pltpu.SMEM(arg.shape, arg.dtype) for arg in small_args],
            *[pltpu.VMEM(arg.shape, arg.dtype) for arg in large_args],
            pltpu.SemaphoreType.DMA((8,)),
        ),
    )
    gathered = local
    masks = [1 << bit for bit in range(side_size.bit_length() - 1)]
    for mask in masks:
        shape = (2 * gathered.shape[0], gathered.shape[1])
        gathered = call(
            join_kernel,
            jax.ShapeDtypeStruct(shape, gathered.dtype),
            [VMEM] * 2,
            (gathered, swap(gathered, "side", mask)),
            limit=small,
        )
    other = swap(gathered, "tp", 1)
    slots, depth = 6, 256
    held = pltpu.VMEM((width, half), w_down.dtype)
    hidden, down_own = call(
        hidden_kernel,
        (jax.ShapeDtypeStruct((rows, width), jnp.bfloat16), held),
        [SMEM] + [VMEM] * 4 + [ANY] * 2,
        (where, gathered, other, norm_gain, in_vmem(w_gate), in_hbm(w_up), in_hbm(w_down)),
        (
            pltpu.VMEM((rows, 2 * half), jnp.bfloat16),
            pltpu.VMEM((rows, width), jnp.float32),
            pltpu.VMEM((slots, depth, width), jnp.bfloat16),
            pltpu.SemaphoreType.DMA((slots,)),
            pltpu.SemaphoreType.DMA,
        ),
        small + slots * depth * width * 2,
    )
    hidden_other = swap(hidden, "tp", 1)
    part, down_other = call(
        down_own_kernel,
        (jax.ShapeDtypeStruct((rows, half), jnp.float32), held),
        [SMEM] + [VMEM] * 2 + [ANY],
        (where, hidden, in_vmem(down_own), in_hbm(w_down)),
        (pltpu.SemaphoreType.DMA,),
        small,
    )
    sent = call(
        down_other_kernel,
        jax.ShapeDtypeStruct((rows, half), jnp.bfloat16),
        [SMEM] + [VMEM] * 4,
        (where, hidden_other, part, gathered, in_vmem(down_other)),
        limit=small,
    )
    for mask in reversed(masks):
        count = sent.shape[0] // 2
        received = swap(sent[count:], "side", mask)
        if mask > 1:
            sent = sent[:count].astype(jnp.float32) + received.astype(jnp.float32)
            sent = sent.astype(jnp.bfloat16)
    return call(
        final_kernel,
        jax.ShapeDtypeStruct(residual.shape, residual.dtype),
        [VMEM] * 3,
        (local, sent, received),
    )


def solution(mesh):
    in_specs = (
        P(None, ("groups", "side"), "tp"),
        P(None, ("groups", "side"), "tp"),
        P(("groups", "side"), None, "tp"),
        P(("groups", "side"), None, "tp"),
        P(None, ("groups", "side"), None),
        P(None, ("groups", "side")),
        P(None, ("groups", "side"), None),
        P(None, ("groups", "side")),
        P(),
        P(None, ("side", "tp")),
        P(None, ("side", "tp")),
        P("side", "tp"),
    )
    out_specs = P(None, ("groups", "side"), "tp")
    return jax.shard_map(
        per_device, mesh=mesh, in_specs=in_specs, out_specs=out_specs, check_vma=False
    )
```

```python
import functools
import math

import jax
import jax.numpy as jnp
from jax import lax
from jax.experimental import pallas as pl
from jax.experimental.pallas import tpu as pltpu
from jax.sharding import PartitionSpec as P

HEAD_DIM = 128
EXPERTS = 4
EPS = 1e-05
GATE_ONE = 65536.0
LANES = 128
DOWN_TILES = 3
SMALL = 2 << 20


def by_row(shape, scalars):
    token = lax.broadcasted_iota(jnp.int32, shape, 0) % len(scalars)
    out = jnp.full(shape, scalars[0])
    for idx in range(1, len(scalars)):
        out = jnp.where(token == idx, scalars[idx], out)
    return out


def flat(ref):
    return jnp.concatenate([ref[idx].astype(jnp.float32) for idx in range(ref.shape[0])], axis=0)


def attend_kernel(*refs):
    count = 8
    _where, sources, buffers = refs[0], refs[1 : 1 + count], refs[-1 - count : -1]
    out_ref, sem = refs[-2 - count], refs[-1]
    copies = [
        pltpu.make_async_copy(source, buffer, sem.at[idx])
        for idx, (source, buffer) in enumerate(zip(sources, buffers))
    ]
    for copy in copies:
        copy.start()
    for copy in copies:
        copy.wait()
    pages_ref, len_ref, routes_ref, gate_ref, res_ref, q_ref, k_ref, v_ref = buffers
    micro, dev, half = res_ref.shape
    tok = micro * dev
    pages, page, kv_width = k_ref.shape
    kv_local = kv_width // HEAD_DIM
    group = half // kv_width
    inv_root = 1.0 / math.sqrt(HEAD_DIM)
    keys = k_ref[...].reshape(pages * page, kv_width)
    values = v_ref[...].reshape(pages * page, kv_width)
    shape = (group * tok, pages * page)
    slot = lax.broadcasted_iota(jnp.int32, shape, 1)
    slot_page, offset = slot // page, slot % page
    position = jnp.full(shape, 1 << 20, jnp.int32)
    for nth in range(pages_ref.shape[2]):
        owner = by_row(shape, [pages_ref[t // dev, t % dev, nth] for t in range(tok)])
        position = jnp.where(slot_page == owner, offset + nth * page, position)
    live = position < by_row(shape, [len_ref[t // dev, t % dev] for t in range(tok)])
    queries = flat(q_ref)
    residual = flat(res_ref)
    for head in range(kv_local):
        cols = slice(head * HEAD_DIM, (head + 1) * HEAD_DIM)
        first = head * group
        rows = jnp.concatenate(
            [
                queries[:, (first + g) * HEAD_DIM : (first + g + 1) * HEAD_DIM]
                for g in range(group)
            ],
            axis=0,
        ).astype(jnp.bfloat16)
        scores = lax.dot_general(
            rows, keys[:, cols], (((1,), (1,)), ((), ())), preferred_element_type=jnp.float32
        )
        scores = jnp.where(live, scores * inv_root, -1e30)
        row_max = jnp.max(scores, axis=-1, keepdims=True)
        unnorm = jnp.where(live, jnp.exp(scores - row_max), 0.0)
        denom = jnp.sum(unnorm, axis=-1, keepdims=True)
        blended = (
            jnp.dot(
                unnorm.astype(jnp.bfloat16), values[:, cols], preferred_element_type=jnp.float32
            )
            / denom
        )
        for g in range(group):
            at = slice((first + g) * HEAD_DIM, (first + g + 1) * HEAD_DIM)
            carried = residual[:, at] + blended[g * tok : (g + 1) * tok]
            out_ref[:, at] = carried.astype(jnp.bfloat16)
    lane = lax.broadcasted_iota(jnp.int32, (tok, LANES), 1)
    expert = lane % EXPERTS
    fixed = by_row((tok, LANES), [gate_ref[t // dev, t % dev] for t in range(tok)])
    one = by_row((tok, LANES), [routes_ref[t // dev, t % dev, 0] for t in range(tok)])
    two = by_row((tok, LANES), [routes_ref[t // dev, t % dev, 1] for t in range(tok)])
    fixed = fixed.astype(jnp.float32)
    weight = jnp.where(expert == one, fixed / GATE_ONE, 0.0) + jnp.where(
        expert == two, (GATE_ONE - fixed) / GATE_ONE, 0.0
    )
    high = weight.astype(jnp.bfloat16).astype(jnp.float32)
    mid = (weight - high).astype(jnp.bfloat16).astype(jnp.float32)
    low = weight - high - mid
    term = lane // EXPERTS
    packed = jnp.where(
        term == 0, high, jnp.where(term == 1, mid, jnp.where(term == 2, low, 0.0))
    )
    out_ref[:, half:] = packed.astype(jnp.bfloat16)


def join_kernel(one_ref, two_ref, out_ref):
    out_ref[...] = jnp.concatenate([one_ref[...], two_ref[...]], axis=0)


def half_copy(w_ref, out_ref, which, sem):
    depth = out_ref.shape[0]
    start = pl.multiple_of(which * depth, depth)
    return pltpu.make_async_copy(w_ref.at[pl.ds(start, depth), :], out_ref, sem)


def hidden_kernel(
    where_ref,
    own_ref,
    other_ref,
    gain_ref,
    wg_ref,
    wu_ref,
    wd_ref,
    out_ref,
    down_ref,
    x_ref,
    gate_ref,
    buf_ref,
    sem,
    down_sem,
):
    slots, _, tile = buf_ref.shape
    half = own_ref.shape[1] - LANES
    chunks = out_ref.shape[1] // tile
    down = half_copy(wd_ref, down_ref, where_ref[0], down_sem)

    def columns(idx):
        return pl.ds(pl.multiple_of(idx * tile, tile), tile)

    def up_copy(idx):
        slot = lax.rem(idx, slots)
        return pltpu.make_async_copy(wu_ref.at[:, columns(idx)], buf_ref.at[slot], sem.at[slot])

    lax.fori_loop(0, slots, lambda idx, _: up_copy(idx).start(), None)
    is_first = where_ref[0] == 0
    own = own_ref[:, :half].astype(jnp.float32)
    other = other_ref[:, :half].astype(jnp.float32)
    square = jnp.sum(own * own, axis=-1, keepdims=True)
    square = square + jnp.sum(other * other, axis=-1, keepdims=True)
    inv_rms = lax.rsqrt(square / (2 * half) + EPS)
    left = jnp.where(is_first, own, other)
    right = jnp.where(is_first, other, own)
    gain = gain_ref[...].astype(jnp.float32).reshape(1, -1)
    x_ref[:, :half] = (left * inv_rms * gain[:, :half]).astype(jnp.bfloat16)
    x_ref[:, half:] = (right * inv_rms * gain[:, half:]).astype(jnp.bfloat16)

    def gate_step(idx, _):
        at = columns(idx)
        gate = jnp.dot(x_ref[...], wg_ref[:, at], preferred_element_type=jnp.float32)
        gate_ref[:, at] = gate / (1.0 + jnp.exp(-gate))

    lax.fori_loop(0, chunks, gate_step, None)

    def up_step(idx, _):
        up_copy(idx).wait()
        up = jnp.dot(
            x_ref[...], buf_ref[lax.rem(idx, slots)], preferred_element_type=jnp.float32
        )
        at = columns(idx)
        out_ref[:, at] = (gate_ref[:, at] * up).astype(jnp.bfloat16)

        @pl.when(idx + slots < chunks)
        def _():
            up_copy(idx + slots).start()

        @pl.when(idx + slots == chunks)
        def _():
            down.start()

    lax.fori_loop(0, chunks, up_step, None)
    down.wait()


def down_own_kernel(where_ref, hid_ref, own_ref, w_ref, out_ref, other_ref, sem):
    tile = out_ref.shape[1] // DOWN_TILES
    copy = half_copy(w_ref, other_ref, 1 - where_ref[0], sem)
    copy.start()

    def step(idx, _):
        at = pl.ds(pl.multiple_of(idx * tile, tile), tile)
        out_ref[:, at] = jnp.dot(hid_ref[...], own_ref[:, at], preferred_element_type=jnp.float32)

    lax.fori_loop(0, DOWN_TILES, step, None)
    copy.wait()


def down_other_kernel(where_ref, hid_ref, part_ref, extra_ref, w_ref, out_ref):
    total = part_ref[...] + jnp.dot(
        hid_ref[...], w_ref[...], preferred_element_type=jnp.float32
    )
    extra = extra_ref[:, -LANES:].astype(jnp.float32)
    lane = lax.broadcasted_iota(jnp.int32, extra.shape, 1)
    mine = (lane % EXPERTS == where_ref[1]) & (lane < 3 * EXPERTS)
    weight = jnp.sum(jnp.where(mine, extra, 0.0), axis=-1, keepdims=True)
    out_ref[...] = (total * weight).astype(jnp.bfloat16)


def final_kernel(carried_ref, mine_ref, received_ref, out_ref):
    micro, dev, half = out_ref.shape
    total = carried_ref[:, :half].astype(jnp.float32)
    total = total + (
        mine_ref[: micro * dev].astype(jnp.float32) + received_ref[...].astype(jnp.float32)
    )
    for idx in range(micro):
        out_ref[idx] = total[idx * dev : (idx + 1) * dev].astype(jnp.bfloat16)


SMEM = pl.BlockSpec(memory_space=pltpu.SMEM)
VMEM = pl.BlockSpec(memory_space=pltpu.VMEM)
ANY = pl.BlockSpec(memory_space=pl.ANY)


def call(kernel, out_shape, in_specs, args, scratch=(), limit=SMALL):
    return pl.pallas_call(
        kernel,
        out_shape=out_shape,
        in_specs=in_specs,
        out_specs=[VMEM] * len(out_shape) if isinstance(out_shape, tuple) else VMEM,
        scratch_shapes=scratch,
        compiler_params=pltpu.CompilerParams(vmem_limit_bytes=limit),
    )(*args)


def in_vmem(array):
    return pltpu.with_memory_space_constraint(array, pltpu.VMEM)


def in_hbm(array):
    return pltpu.with_memory_space_constraint(array, pltpu.HBM)


def swap(array, axis, mask):
    size = lax.axis_size(axis)
    return lax.ppermute(array, axis, [(i, i ^ mask) for i in range(size)])


def per_device(
    residual,
    queries,
    key_cache,
    value_cache,
    page_table,
    lengths,
    routes,
    gate_fixed,
    norm_gain,
    w_gate,
    w_up,
    w_down,
):
    micro_count, tok_dev, half = residual.shape
    side_size = lax.axis_size("side")
    tok = micro_count * tok_dev
    rows = tok * side_size
    span = side_size // EXPERTS
    small = SMALL + 64 * rows * half
    width = w_gate.shape[1]
    where = jnp.stack([lax.axis_index("tp"), lax.axis_index("side") // span]).astype(jnp.int32)
    small_args = (page_table, lengths, routes, gate_fixed)
    large_args = (residual, queries, key_cache, value_cache)
    local = call(
        attend_kernel,
        jax.ShapeDtypeStruct((tok, half + LANES), jnp.bfloat16),
        [SMEM] + [ANY] * 10,
        (where, *[in_hbm(arg) for arg in (*small_args, *large_args, w_gate, w_up)]),
        (
            *[pltpu.SMEM(arg.shape, arg.dtype) for arg in small_args],
            *[pltpu.VMEM(arg.shape, arg.dtype) for arg in large_args],
            pltpu.SemaphoreType.DMA((8,)),
        ),
    )
    gathered = local
    masks = [1 << bit for bit in range(side_size.bit_length() - 1)]
    for mask in masks:
        shape = (2 * gathered.shape[0], gathered.shape[1])
        gathered = call(
            join_kernel,
            jax.ShapeDtypeStruct(shape, gathered.dtype),
            [VMEM] * 2,
            (gathered, swap(gathered, "side", mask)),
            limit=small,
        )
    other = swap(gathered, "tp", 1)
    tile = math.gcd(width, 512)
    slots = min(width // tile, 6)
    held = pltpu.VMEM((width, half), w_down.dtype)
    hidden, down_own = call(
        hidden_kernel,
        (jax.ShapeDtypeStruct((rows, width), jnp.bfloat16), held),
        [SMEM] + [VMEM] * 4 + [ANY] * 2,
        (where, gathered, other, norm_gain, in_vmem(w_gate), in_hbm(w_up), in_hbm(w_down)),
        (
            pltpu.VMEM((rows, 2 * half), jnp.bfloat16),
            pltpu.VMEM((rows, width), jnp.float32),
            pltpu.VMEM((slots, 2 * half, tile), jnp.bfloat16),
            pltpu.SemaphoreType.DMA((slots,)),
            pltpu.SemaphoreType.DMA,
        ),
        small + slots * half * tile * 4,
    )
    hidden_other = swap(hidden, "tp", 1)
    part, down_other = call(
        down_own_kernel,
        (jax.ShapeDtypeStruct((rows, half), jnp.float32), held),
        [SMEM] + [VMEM] * 2 + [ANY],
        (where, hidden, in_vmem(down_own), in_hbm(w_down)),
        (pltpu.SemaphoreType.DMA,),
        small,
    )
    sent = call(
        down_other_kernel,
        jax.ShapeDtypeStruct((rows, half), jnp.bfloat16),
        [SMEM] + [VMEM] * 4,
        (where, hidden_other, part, gathered, in_vmem(down_other)),
        limit=small,
    )
    for mask in reversed(masks):
        count = sent.shape[0] // 2
        received = swap(sent[count:], "side", mask)
        if mask > 1:
            sent = sent[:count].astype(jnp.float32) + received.astype(jnp.float32)
            sent = sent.astype(jnp.bfloat16)
    return call(
        final_kernel,
        jax.ShapeDtypeStruct(residual.shape, residual.dtype),
        [VMEM] * 3,
        (local, sent, received),
    )


def solution(mesh):
    in_specs = (
        P(None, ("groups", "side"), "tp"),
        P(None, ("groups", "side"), "tp"),
        P(("groups", "side"), None, "tp"),
        P(("groups", "side"), None, "tp"),
        P(None, ("groups", "side"), None),
        P(None, ("groups", "side")),
        P(None, ("groups", "side"), None),
        P(None, ("groups", "side")),
        P(),
        P(None, ("side", "tp")),
        P(None, ("side", "tp")),
        P("side", "tp"),
    )
    out_specs = P(None, ("groups", "side"), "tp")
    return jax.shard_map(
        per_device, mesh=mesh, in_specs=in_specs, out_specs=out_specs, check_vma=False
    )
```

```python
import functools
import math

import jax
import jax.numpy as jnp
from jax import lax
from jax.experimental import pallas as pl
from jax.experimental.pallas import tpu as pltpu
from jax.sharding import PartitionSpec as P

HEAD_DIM = 128
EXPERTS = 4
EPS = 1e-05
GATE_ONE = 65536.0
LANES = 128
DOWN_TILES = 3
SMALL = 2 << 20


def by_row(shape, scalars):
    token = lax.broadcasted_iota(jnp.int32, shape, 0) % len(scalars)
    out = jnp.full(shape, scalars[0])
    for idx in range(1, len(scalars)):
        out = jnp.where(token == idx, scalars[idx], out)
    return out


def flat(ref):
    return jnp.concatenate([ref[idx].astype(jnp.float32) for idx in range(ref.shape[0])], axis=0)


def attend_kernel(*refs):
    count = 8
    _where, sources, buffers = refs[0], refs[1 : 1 + count], refs[-1 - count : -1]
    out_ref, sem = refs[-2 - count], refs[-1]
    copies = [
        pltpu.make_async_copy(source, buffer, sem.at[idx])
        for idx, (source, buffer) in enumerate(zip(sources, buffers))
    ]
    for copy in copies:
        copy.start()
    for copy in copies:
        copy.wait()
    pages_ref, len_ref, routes_ref, gate_ref, res_ref, q_ref, k_ref, v_ref = buffers
    micro, dev, half = res_ref.shape
    tok = micro * dev
    pages, page, kv_width = k_ref.shape
    kv_local = kv_width // HEAD_DIM
    group = half // kv_width
    inv_root = 1.0 / math.sqrt(HEAD_DIM)
    keys = k_ref[...].reshape(pages * page, kv_width)
    values = v_ref[...].reshape(pages * page, kv_width)
    shape = (group * tok, pages * page)
    slot = lax.broadcasted_iota(jnp.int32, shape, 1)
    slot_page, offset = slot // page, slot % page
    position = jnp.full(shape, 1 << 20, jnp.int32)
    for nth in range(pages_ref.shape[2]):
        owner = by_row(shape, [pages_ref[t // dev, t % dev, nth] for t in range(tok)])
        position = jnp.where(slot_page == owner, offset + nth * page, position)
    live = position < by_row(shape, [len_ref[t // dev, t % dev] for t in range(tok)])
    queries = flat(q_ref)
    residual = flat(res_ref)
    for head in range(kv_local):
        cols = slice(head * HEAD_DIM, (head + 1) * HEAD_DIM)
        first = head * group
        rows = jnp.concatenate(
            [
                queries[:, (first + g) * HEAD_DIM : (first + g + 1) * HEAD_DIM]
                for g in range(group)
            ],
            axis=0,
        ).astype(jnp.bfloat16)
        scores = lax.dot_general(
            rows, keys[:, cols], (((1,), (1,)), ((), ())), preferred_element_type=jnp.float32
        )
        scores = jnp.where(live, scores * inv_root, -1e30)
        row_max = jnp.max(scores, axis=-1, keepdims=True)
        unnorm = jnp.where(live, jnp.exp(scores - row_max), 0.0)
        denom = jnp.sum(unnorm, axis=-1, keepdims=True)
        blended = (
            jnp.dot(
                unnorm.astype(jnp.bfloat16), values[:, cols], preferred_element_type=jnp.float32
            )
            / denom
        )
        for g in range(group):
            at = slice((first + g) * HEAD_DIM, (first + g + 1) * HEAD_DIM)
            carried = residual[:, at] + blended[g * tok : (g + 1) * tok]
            out_ref[:, at] = carried.astype(jnp.bfloat16)
    lane = lax.broadcasted_iota(jnp.int32, (tok, LANES), 1)
    expert = lane % EXPERTS
    fixed = by_row((tok, LANES), [gate_ref[t // dev, t % dev] for t in range(tok)])
    one = by_row((tok, LANES), [routes_ref[t // dev, t % dev, 0] for t in range(tok)])
    two = by_row((tok, LANES), [routes_ref[t // dev, t % dev, 1] for t in range(tok)])
    fixed = fixed.astype(jnp.float32)
    weight = jnp.where(expert == one, fixed / GATE_ONE, 0.0) + jnp.where(
        expert == two, (GATE_ONE - fixed) / GATE_ONE, 0.0
    )
    high = weight.astype(jnp.bfloat16).astype(jnp.float32)
    mid = (weight - high).astype(jnp.bfloat16).astype(jnp.float32)
    low = weight - high - mid
    term = lane // EXPERTS
    packed = jnp.where(
        term == 0, high, jnp.where(term == 1, mid, jnp.where(term == 2, low, 0.0))
    )
    out_ref[:, half:] = packed.astype(jnp.bfloat16)


def join_kernel(one_ref, two_ref, out_ref):
    out_ref[...] = jnp.concatenate([one_ref[...], two_ref[...]], axis=0)


def half_copy(w_ref, out_ref, which, sem):
    depth = out_ref.shape[0]
    start = pl.multiple_of(which * depth, depth)
    return pltpu.make_async_copy(w_ref.at[pl.ds(start, depth), :], out_ref, sem)


def hidden_kernel(
    where_ref,
    own_ref,
    other_ref,
    gain_ref,
    wg_ref,
    wu_ref,
    wd_ref,
    out_ref,
    down_ref,
    x_ref,
    gate_ref,
    buf_ref,
    sem,
    down_sem,
):
    slots, _, tile = buf_ref.shape
    half = own_ref.shape[1] - LANES
    chunks = out_ref.shape[1] // tile
    down = half_copy(wd_ref, down_ref, where_ref[0], down_sem)

    def columns(idx):
        return pl.ds(pl.multiple_of(idx * tile, tile), tile)

    def up_copy(idx):
        slot = lax.rem(idx, slots)
        return pltpu.make_async_copy(wu_ref.at[:, columns(idx)], buf_ref.at[slot], sem.at[slot])

    lax.fori_loop(0, slots, lambda idx, _: up_copy(idx).start(), None)
    is_first = where_ref[0] == 0
    own = own_ref[:, :half].astype(jnp.float32)
    other = other_ref[:, :half].astype(jnp.float32)
    square = jnp.sum(own * own, axis=-1, keepdims=True)
    square = square + jnp.sum(other * other, axis=-1, keepdims=True)
    inv_rms = lax.rsqrt(square / (2 * half) + EPS)
    left = jnp.where(is_first, own, other)
    right = jnp.where(is_first, other, own)
    gain = gain_ref[...].astype(jnp.float32).reshape(1, -1)
    x_ref[:, :half] = (left * inv_rms * gain[:, :half]).astype(jnp.bfloat16)
    x_ref[:, half:] = (right * inv_rms * gain[:, half:]).astype(jnp.bfloat16)

    def gate_step(idx, _):
        at = columns(idx)
        gate = jnp.dot(x_ref[...], wg_ref[:, at], preferred_element_type=jnp.float32)
        gate_ref[:, at] = gate / (1.0 + jnp.exp(-gate))

    lax.fori_loop(0, chunks, gate_step, None)

    def up_step(idx, _):
        up_copy(idx).wait()
        up = jnp.dot(
            x_ref[...], buf_ref[lax.rem(idx, slots)], preferred_element_type=jnp.float32
        )
        at = columns(idx)
        out_ref[:, at] = (gate_ref[:, at] * up).astype(jnp.bfloat16)

        @pl.when(idx + slots < chunks)
        def _():
            up_copy(idx + slots).start()

        @pl.when(idx + slots == chunks)
        def _():
            down.start()

    lax.fori_loop(0, chunks, up_step, None)
    down.wait()


def down_own_kernel(where_ref, hid_ref, own_ref, w_ref, out_ref, other_ref, sem):
    tile = out_ref.shape[1] // DOWN_TILES
    copy = half_copy(w_ref, other_ref, 1 - where_ref[0], sem)
    copy.start()

    def step(idx, _):
        at = pl.ds(pl.multiple_of(idx * tile, tile), tile)
        out_ref[:, at] = jnp.dot(hid_ref[...], own_ref[:, at], preferred_element_type=jnp.float32)

    lax.fori_loop(0, DOWN_TILES, step, None)
    copy.wait()


def down_other_kernel(where_ref, hid_ref, part_ref, extra_ref, w_ref, out_ref):
    total = part_ref[...] + jnp.dot(
        hid_ref[...], w_ref[...], preferred_element_type=jnp.float32
    )
    extra = extra_ref[:, -LANES:].astype(jnp.float32)
    lane = lax.broadcasted_iota(jnp.int32, extra.shape, 1)
    mine = (lane % EXPERTS == where_ref[1]) & (lane < 3 * EXPERTS)
    weight = jnp.sum(jnp.where(mine, extra, 0.0), axis=-1, keepdims=True)
    total = total * weight
    blocks, tok, _ = out_ref.shape
    for idx in range(blocks):
        out_ref[where_ref[2] ^ idx] = total[idx * tok : (idx + 1) * tok].astype(jnp.bfloat16)


def final_kernel(carried_ref, received_ref, out_ref):
    micro, dev, half = out_ref.shape
    moe = received_ref[0].astype(jnp.float32)
    for idx in range(1, received_ref.shape[0]):
        moe = moe + received_ref[idx].astype(jnp.float32)
    total = carried_ref[:, :half].astype(jnp.float32) + moe
    for idx in range(micro):
        out_ref[idx] = total[idx * dev : (idx + 1) * dev].astype(jnp.bfloat16)


SMEM = pl.BlockSpec(memory_space=pltpu.SMEM)
VMEM = pl.BlockSpec(memory_space=pltpu.VMEM)
ANY = pl.BlockSpec(memory_space=pl.ANY)


def call(kernel, out_shape, in_specs, args, scratch=(), limit=SMALL):
    return pl.pallas_call(
        kernel,
        out_shape=out_shape,
        in_specs=in_specs,
        out_specs=[VMEM] * len(out_shape) if isinstance(out_shape, tuple) else VMEM,
        scratch_shapes=scratch,
        compiler_params=pltpu.CompilerParams(vmem_limit_bytes=limit),
    )(*args)


def in_vmem(array):
    return pltpu.with_memory_space_constraint(array, pltpu.VMEM)


def in_hbm(array):
    return pltpu.with_memory_space_constraint(array, pltpu.HBM)


def swap(array, axis, mask):
    size = lax.axis_size(axis)
    return lax.ppermute(array, axis, [(i, i ^ mask) for i in range(size)])


def per_device(
    residual,
    queries,
    key_cache,
    value_cache,
    page_table,
    lengths,
    routes,
    gate_fixed,
    norm_gain,
    w_gate,
    w_up,
    w_down,
):
    micro_count, tok_dev, half = residual.shape
    side_size = lax.axis_size("side")
    tok = micro_count * tok_dev
    rows = tok * side_size
    span = side_size // EXPERTS
    small = SMALL + 64 * rows * half
    width = w_gate.shape[1]
    side = lax.axis_index("side")
    where = jnp.stack([lax.axis_index("tp"), side // span, side]).astype(jnp.int32)
    small_args = (page_table, lengths, routes, gate_fixed)
    large_args = (residual, queries, key_cache, value_cache)
    local = call(
        attend_kernel,
        jax.ShapeDtypeStruct((tok, half + LANES), jnp.bfloat16),
        [SMEM] + [ANY] * 10,
        (where, *[in_hbm(arg) for arg in (*small_args, *large_args, w_gate, w_up)]),
        (
            *[pltpu.SMEM(arg.shape, arg.dtype) for arg in small_args],
            *[pltpu.VMEM(arg.shape, arg.dtype) for arg in large_args],
            pltpu.SemaphoreType.DMA((8,)),
        ),
    )
    gathered = local
    masks = [1 << bit for bit in range(side_size.bit_length() - 1)]
    for mask in masks:
        shape = (2 * gathered.shape[0], gathered.shape[1])
        gathered = call(
            join_kernel,
            jax.ShapeDtypeStruct(shape, gathered.dtype),
            [VMEM] * 2,
            (gathered, swap(gathered, "side", mask)),
            limit=small,
        )
    other = swap(gathered, "tp", 1)
    tile = math.gcd(width, 512)
    slots = min(width // tile, 6)
    held = pltpu.VMEM((width, half), w_down.dtype)
    hidden, down_own = call(
        hidden_kernel,
        (pltpu.VMEM((rows, width), jnp.bfloat16), held),
        [SMEM] + [VMEM] * 4 + [ANY] * 2,
        (where, in_vmem(gathered), in_vmem(other), norm_gain, in_vmem(w_gate), in_hbm(w_up), in_hbm(w_down)),
        (
            pltpu.VMEM((rows, 2 * half), jnp.bfloat16),
            pltpu.VMEM((rows, width), jnp.float32),
            pltpu.VMEM((slots, 2 * half, tile), jnp.bfloat16),
            pltpu.SemaphoreType.DMA((slots,)),
            pltpu.SemaphoreType.DMA,
        ),
        SMALL + rows * half * 24 + slots * half * tile * 4,
    )
    hidden_other = swap(hidden, "tp", 1)
    part, down_other = call(
        down_own_kernel,
        (jax.ShapeDtypeStruct((rows, half), jnp.float32), held),
        [SMEM] + [VMEM] * 2 + [ANY],
        (where, in_vmem(hidden), in_vmem(down_own), in_hbm(w_down)),
        (pltpu.SemaphoreType.DMA,),
        small,
    )
    sent = call(
        down_other_kernel,
        jax.ShapeDtypeStruct((side_size, tok, half), jnp.bfloat16),
        [SMEM] + [VMEM] * 4,
        (where, hidden_other, part, gathered, in_vmem(down_other)),
        limit=small,
    )
    received = lax.all_to_all(sent, "side", split_axis=0, concat_axis=0, tiled=True)
    return call(
        final_kernel,
        jax.ShapeDtypeStruct(residual.shape, residual.dtype),
        [VMEM] * 2,
        (local, received),
        limit=small,
    )


def solution(mesh):
    in_specs = (
        P(None, ("groups", "side"), "tp"),
        P(None, ("groups", "side"), "tp"),
        P(("groups", "side"), None, "tp"),
        P(("groups", "side"), None, "tp"),
        P(None, ("groups", "side"), None),
        P(None, ("groups", "side")),
        P(None, ("groups", "side"), None),
        P(None, ("groups", "side")),
        P(),
        P(None, ("side", "tp")),
        P(None, ("side", "tp")),
        P("side", "tp"),
    )
    out_specs = P(None, ("groups", "side"), "tp")
    return jax.shard_map(
        per_device, mesh=mesh, in_specs=in_specs, out_specs=out_specs, check_vma=False
    )
```

```python
import functools
import math

import jax
import jax.numpy as jnp
from jax import lax
from jax.experimental import pallas as pl
from jax.experimental.pallas import tpu as pltpu
from jax.sharding import PartitionSpec as P

HEAD_DIM = 128
EXPERTS = 4
EPS = 1e-05
GATE_ONE = 65536.0
LANES = 128
DOWN_TILES = 3
SMALL = 2 << 20


def by_row(shape, scalars):
    token = lax.broadcasted_iota(jnp.int32, shape, 0) % len(scalars)
    out = jnp.full(shape, scalars[0])
    for idx in range(1, len(scalars)):
        out = jnp.where(token == idx, scalars[idx], out)
    return out


def flat(ref):
    return jnp.concatenate([ref[idx].astype(jnp.float32) for idx in range(ref.shape[0])], axis=0)


def attend_kernel(*refs):
    count = 8
    _where, sources, buffers = refs[0], refs[1 : 1 + count], refs[-1 - count : -1]
    out_ref, sem = refs[-2 - count], refs[-1]
    copies = [
        pltpu.make_async_copy(source, buffer, sem.at[idx])
        for idx, (source, buffer) in enumerate(zip(sources, buffers))
    ]
    for copy in copies:
        copy.start()
    for copy in copies:
        copy.wait()
    pages_ref, len_ref, routes_ref, gate_ref, res_ref, q_ref, k_ref, v_ref = buffers
    micro, dev, half = res_ref.shape
    tok = micro * dev
    pages, page, kv_width = k_ref.shape
    kv_local = kv_width // HEAD_DIM
    group = half // kv_width
    inv_root = 1.0 / math.sqrt(HEAD_DIM)
    keys = k_ref[...].reshape(pages * page, kv_width)
    values = v_ref[...].reshape(pages * page, kv_width)
    shape = (group * tok, pages * page)
    slot = lax.broadcasted_iota(jnp.int32, shape, 1)
    slot_page, offset = slot // page, slot % page
    position = jnp.full(shape, 1 << 20, jnp.int32)
    for nth in range(pages_ref.shape[2]):
        owner = by_row(shape, [pages_ref[t // dev, t % dev, nth] for t in range(tok)])
        position = jnp.where(slot_page == owner, offset + nth * page, position)
    live = position < by_row(shape, [len_ref[t // dev, t % dev] for t in range(tok)])
    queries = flat(q_ref)
    residual = flat(res_ref)
    for head in range(kv_local):
        cols = slice(head * HEAD_DIM, (head + 1) * HEAD_DIM)
        first = head * group
        rows = jnp.concatenate(
            [
                queries[:, (first + g) * HEAD_DIM : (first + g + 1) * HEAD_DIM]
                for g in range(group)
            ],
            axis=0,
        ).astype(jnp.bfloat16)
        scores = lax.dot_general(
            rows, keys[:, cols], (((1,), (1,)), ((), ())), preferred_element_type=jnp.float32
        )
        scores = jnp.where(live, scores * inv_root, -1e30)
        row_max = jnp.max(scores, axis=-1, keepdims=True)
        unnorm = jnp.where(live, jnp.exp(scores - row_max), 0.0)
        denom = jnp.sum(unnorm, axis=-1, keepdims=True)
        blended = (
            jnp.dot(
                unnorm.astype(jnp.bfloat16), values[:, cols], preferred_element_type=jnp.float32
            )
            / denom
        )
        for g in range(group):
            at = slice((first + g) * HEAD_DIM, (first + g + 1) * HEAD_DIM)
            carried = residual[:, at] + blended[g * tok : (g + 1) * tok]
            out_ref[0, :, at] = carried.astype(jnp.bfloat16)
    lane = lax.broadcasted_iota(jnp.int32, (tok, LANES), 1)
    expert = lane % EXPERTS
    fixed = by_row((tok, LANES), [gate_ref[t // dev, t % dev] for t in range(tok)])
    one = by_row((tok, LANES), [routes_ref[t // dev, t % dev, 0] for t in range(tok)])
    two = by_row((tok, LANES), [routes_ref[t // dev, t % dev, 1] for t in range(tok)])
    fixed = fixed.astype(jnp.float32)
    weight = jnp.where(expert == one, fixed / GATE_ONE, 0.0) + jnp.where(
        expert == two, (GATE_ONE - fixed) / GATE_ONE, 0.0
    )
    high = weight.astype(jnp.bfloat16).astype(jnp.float32)
    mid = (weight - high).astype(jnp.bfloat16).astype(jnp.float32)
    low = weight - high - mid
    term = lane // EXPERTS
    packed = jnp.where(
        term == 0, high, jnp.where(term == 1, mid, jnp.where(term == 2, low, 0.0))
    )
    out_ref[0, :, half:] = packed.astype(jnp.bfloat16)
    for idx in range(1, out_ref.shape[0]):
        out_ref[idx] = out_ref[0]


def half_copy(w_ref, out_ref, which, sem):
    depth = out_ref.shape[0]
    start = pl.multiple_of(which * depth, depth)
    return pltpu.make_async_copy(w_ref.at[pl.ds(start, depth), :], out_ref, sem)


def hidden_kernel(
    where_ref,
    own_ref,
    other_ref,
    gain_ref,
    wg_ref,
    wu_ref,
    wd_ref,
    out_ref,
    down_ref,
    x_ref,
    gate_ref,
    buf_ref,
    sem,
    down_sem,
):
    slots, _, tile = buf_ref.shape
    half = own_ref.shape[2] - LANES
    chunks = out_ref.shape[1] // tile
    down = half_copy(wd_ref, down_ref, where_ref[0], down_sem)

    def columns(idx):
        return pl.ds(pl.multiple_of(idx * tile, tile), tile)

    def up_copy(idx):
        slot = lax.rem(idx, slots)
        return pltpu.make_async_copy(wu_ref.at[:, columns(idx)], buf_ref.at[slot], sem.at[slot])

    lax.fori_loop(0, slots, lambda idx, _: up_copy(idx).start(), None)
    is_first = where_ref[0] == 0
    own = flat(own_ref)[:, :half]
    other = flat(other_ref)[:, :half]
    square = jnp.sum(own * own, axis=-1, keepdims=True)
    square = square + jnp.sum(other * other, axis=-1, keepdims=True)
    inv_rms = lax.rsqrt(square / (2 * half) + EPS)
    left = jnp.where(is_first, own, other)
    right = jnp.where(is_first, other, own)
    gain = gain_ref[...].astype(jnp.float32).reshape(1, -1)
    x_ref[:, :half] = (left * inv_rms * gain[:, :half]).astype(jnp.bfloat16)
    x_ref[:, half:] = (right * inv_rms * gain[:, half:]).astype(jnp.bfloat16)

    def gate_step(idx, _):
        at = columns(idx)
        gate = jnp.dot(x_ref[...], wg_ref[:, at], preferred_element_type=jnp.float32)
        gate_ref[:, at] = gate / (1.0 + jnp.exp(-gate))

    lax.fori_loop(0, chunks, gate_step, None)

    def up_step(idx, _):
        up_copy(idx).wait()
        up = jnp.dot(
            x_ref[...], buf_ref[lax.rem(idx, slots)], preferred_element_type=jnp.float32
        )
        at = columns(idx)
        out_ref[:, at] = (gate_ref[:, at] * up).astype(jnp.bfloat16)

        @pl.when(idx + slots < chunks)
        def _():
            up_copy(idx + slots).start()

        @pl.when(idx + slots == chunks)
        def _():
            down.start()

    lax.fori_loop(0, chunks, up_step, None)
    down.wait()


def down_own_kernel(where_ref, hid_ref, own_ref, w_ref, out_ref, other_ref, sem):
    tile = out_ref.shape[1] // DOWN_TILES
    copy = half_copy(w_ref, other_ref, 1 - where_ref[0], sem)
    copy.start()

    def step(idx, _):
        at = pl.ds(pl.multiple_of(idx * tile, tile), tile)
        out_ref[:, at] = jnp.dot(hid_ref[...], own_ref[:, at], preferred_element_type=jnp.float32)

    lax.fori_loop(0, DOWN_TILES, step, None)
    copy.wait()


def down_other_kernel(where_ref, hid_ref, part_ref, extra_ref, w_ref, out_ref):
    total = part_ref[...] + jnp.dot(
        hid_ref[...], w_ref[...], preferred_element_type=jnp.float32
    )
    extra = flat(extra_ref)[:, -LANES:]
    lane = lax.broadcasted_iota(jnp.int32, extra.shape, 1)
    mine = (lane % EXPERTS == where_ref[1]) & (lane < 3 * EXPERTS)
    weight = jnp.sum(jnp.where(mine, extra, 0.0), axis=-1, keepdims=True)
    total = total * weight
    blocks, tok, _ = out_ref.shape
    for idx in range(blocks):
        out_ref[idx] = total[idx * tok : (idx + 1) * tok].astype(jnp.bfloat16)


def final_kernel(carried_ref, received_ref, out_ref):
    micro, dev, half = out_ref.shape
    moe = received_ref[0].astype(jnp.float32)
    for idx in range(1, received_ref.shape[0]):
        moe = moe + received_ref[idx].astype(jnp.float32)
    total = carried_ref[0, :, :half].astype(jnp.float32) + moe
    for idx in range(micro):
        out_ref[idx] = total[idx * dev : (idx + 1) * dev].astype(jnp.bfloat16)


SMEM = pl.BlockSpec(memory_space=pltpu.SMEM)
VMEM = pl.BlockSpec(memory_space=pltpu.VMEM)
ANY = pl.BlockSpec(memory_space=pl.ANY)


def call(kernel, out_shape, in_specs, args, scratch=(), limit=SMALL):
    return pl.pallas_call(
        kernel,
        out_shape=out_shape,
        in_specs=in_specs,
        out_specs=[VMEM] * len(out_shape) if isinstance(out_shape, tuple) else VMEM,
        scratch_shapes=scratch,
        compiler_params=pltpu.CompilerParams(vmem_limit_bytes=limit),
    )(*args)


def in_vmem(array):
    return pltpu.with_memory_space_constraint(array, pltpu.VMEM)


def in_hbm(array):
    return pltpu.with_memory_space_constraint(array, pltpu.HBM)


def swap(array, axis, mask):
    size = lax.axis_size(axis)
    return lax.ppermute(array, axis, [(i, i ^ mask) for i in range(size)])


def per_device(
    residual,
    queries,
    key_cache,
    value_cache,
    page_table,
    lengths,
    routes,
    gate_fixed,
    norm_gain,
    w_gate,
    w_up,
    w_down,
):
    micro_count, tok_dev, half = residual.shape
    side_size = lax.axis_size("side")
    tok = micro_count * tok_dev
    rows = tok * side_size
    span = side_size // EXPERTS
    small = SMALL + 64 * rows * half
    width = w_gate.shape[1]
    where = jnp.stack([lax.axis_index("tp"), lax.axis_index("side") // span]).astype(jnp.int32)
    small_args = (page_table, lengths, routes, gate_fixed)
    large_args = (residual, queries, key_cache, value_cache)
    local = call(
        attend_kernel,
        jax.ShapeDtypeStruct((side_size, tok, half + LANES), jnp.bfloat16),
        [SMEM] + [ANY] * 10,
        (where, *[in_hbm(arg) for arg in (*small_args, *large_args, w_gate, w_up)]),
        (
            *[pltpu.SMEM(arg.shape, arg.dtype) for arg in small_args],
            *[pltpu.VMEM(arg.shape, arg.dtype) for arg in large_args],
            pltpu.SemaphoreType.DMA((8,)),
        ),
        small,
    )
    gathered = lax.all_to_all(local, "side", split_axis=0, concat_axis=0, tiled=True)
    other = swap(gathered, "tp", 1)
    tile = math.gcd(width, 512)
    slots = min(width // tile, 6)
    held = pltpu.VMEM((width, half), w_down.dtype)
    hidden, down_own = call(
        hidden_kernel,
        (pltpu.VMEM((rows, width), jnp.bfloat16), held),
        [SMEM] + [VMEM] * 4 + [ANY] * 2,
        (where, in_vmem(gathered), in_vmem(other), norm_gain, in_vmem(w_gate), in_hbm(w_up), in_hbm(w_down)),
        (
            pltpu.VMEM((rows, 2 * half), jnp.bfloat16),
            pltpu.VMEM((rows, width), jnp.float32),
            pltpu.VMEM((slots, 2 * half, tile), jnp.bfloat16),
            pltpu.SemaphoreType.DMA((slots,)),
            pltpu.SemaphoreType.DMA,
        ),
        SMALL + rows * half * 24 + slots * half * tile * 4,
    )
    hidden_other = swap(hidden, "tp", 1)
    part, down_other = call(
        down_own_kernel,
        (jax.ShapeDtypeStruct((rows, half), jnp.float32), held),
        [SMEM] + [VMEM] * 2 + [ANY],
        (where, in_vmem(hidden), in_vmem(down_own), in_hbm(w_down)),
        (pltpu.SemaphoreType.DMA,),
        small,
    )
    sent = call(
        down_other_kernel,
        jax.ShapeDtypeStruct((side_size, tok, half), jnp.bfloat16),
        [SMEM] + [VMEM] * 4,
        (where, hidden_other, part, gathered, in_vmem(down_other)),
        limit=small,
    )
    received = lax.all_to_all(sent, "side", split_axis=0, concat_axis=0, tiled=True)
    return call(
        final_kernel,
        jax.ShapeDtypeStruct(residual.shape, residual.dtype),
        [VMEM] * 2,
        (local, received),
        limit=small,
    )


def solution(mesh):
    in_specs = (
        P(None, ("groups", "side"), "tp"),
        P(None, ("groups", "side"), "tp"),
        P(("groups", "side"), None, "tp"),
        P(("groups", "side"), None, "tp"),
        P(None, ("groups", "side"), None),
        P(None, ("groups", "side")),
        P(None, ("groups", "side"), None),
        P(None, ("groups", "side")),
        P(),
        P(None, ("side", "tp")),
        P(None, ("side", "tp")),
        P("side", "tp"),
    )
    out_specs = P(None, ("groups", "side"), "tp")
    return jax.shard_map(
        per_device, mesh=mesh, in_specs=in_specs, out_specs=out_specs, check_vma=False
    )
```

```python
import functools
import math

import jax
import jax.numpy as jnp
from jax import lax
from jax.experimental import pallas as pl
from jax.experimental.pallas import tpu as pltpu
from jax.sharding import PartitionSpec as P

HEAD_DIM = 128
EXPERTS = 4
EPS = 1e-05
GATE_ONE = 65536.0
LANES = 128
DOWN_TILES = 3
SMALL = 2 << 20


def by_row(shape, scalars):
    token = lax.broadcasted_iota(jnp.int32, shape, 0) % len(scalars)
    out = jnp.full(shape, scalars[0])
    for idx in range(1, len(scalars)):
        out = jnp.where(token == idx, scalars[idx], out)
    return out


def flat(ref):
    return jnp.concatenate([ref[idx].astype(jnp.float32) for idx in range(ref.shape[0])], axis=0)


def attend_kernel(*refs):
    count = 8
    _where, sources, buffers = refs[0], refs[1 : 1 + count], refs[-1 - count : -1]
    out_ref, sem = refs[-2 - count], refs[-1]
    copies = [
        pltpu.make_async_copy(source, buffer, sem.at[idx])
        for idx, (source, buffer) in enumerate(zip(sources, buffers))
    ]
    for copy in copies:
        copy.start()
    for copy in copies:
        copy.wait()
    pages_ref, len_ref, routes_ref, gate_ref, res_ref, q_ref, k_ref, v_ref = buffers
    micro, dev, half = res_ref.shape
    tok = micro * dev
    pages, page, kv_width = k_ref.shape
    kv_local = kv_width // HEAD_DIM
    group = half // kv_width
    inv_root = 1.0 / math.sqrt(HEAD_DIM)
    keys = k_ref[...].reshape(pages * page, kv_width)
    values = v_ref[...].reshape(pages * page, kv_width)
    shape = (group * tok, pages * page)
    slot = lax.broadcasted_iota(jnp.int32, shape, 1)
    slot_page, offset = slot // page, slot % page
    position = jnp.full(shape, 1 << 20, jnp.int32)
    for nth in range(pages_ref.shape[2]):
        owner = by_row(shape, [pages_ref[t // dev, t % dev, nth] for t in range(tok)])
        position = jnp.where(slot_page == owner, offset + nth * page, position)
    live = position < by_row(shape, [len_ref[t // dev, t % dev] for t in range(tok)])
    queries = flat(q_ref)
    residual = flat(res_ref)
    for head in range(kv_local):
        cols = slice(head * HEAD_DIM, (head + 1) * HEAD_DIM)
        first = head * group
        rows = jnp.concatenate(
            [
                queries[:, (first + g) * HEAD_DIM : (first + g + 1) * HEAD_DIM]
                for g in range(group)
            ],
            axis=0,
        ).astype(jnp.bfloat16)
        scores = lax.dot_general(
            rows, keys[:, cols], (((1,), (1,)), ((), ())), preferred_element_type=jnp.float32
        )
        scores = jnp.where(live, scores * inv_root, -1e30)
        row_max = jnp.max(scores, axis=-1, keepdims=True)
        unnorm = jnp.where(live, jnp.exp(scores - row_max), 0.0)
        denom = jnp.sum(unnorm, axis=-1, keepdims=True)
        blended = (
            jnp.dot(
                unnorm.astype(jnp.bfloat16), values[:, cols], preferred_element_type=jnp.float32
            )
            / denom
        )
        for g in range(group):
            at = slice((first + g) * HEAD_DIM, (first + g + 1) * HEAD_DIM)
            carried = residual[:, at] + blended[g * tok : (g + 1) * tok]
            out_ref[0, :, at] = carried.astype(jnp.bfloat16)
    lane = lax.broadcasted_iota(jnp.int32, (tok, LANES), 1)
    expert = lane % EXPERTS
    fixed = by_row((tok, LANES), [gate_ref[t // dev, t % dev] for t in range(tok)])
    one = by_row((tok, LANES), [routes_ref[t // dev, t % dev, 0] for t in range(tok)])
    two = by_row((tok, LANES), [routes_ref[t // dev, t % dev, 1] for t in range(tok)])
    fixed = fixed.astype(jnp.float32)
    weight = jnp.where(expert == one, fixed / GATE_ONE, 0.0) + jnp.where(
        expert == two, (GATE_ONE - fixed) / GATE_ONE, 0.0
    )
    high = weight.astype(jnp.bfloat16).astype(jnp.float32)
    mid = (weight - high).astype(jnp.bfloat16).astype(jnp.float32)
    low = weight - high - mid
    term = lane // EXPERTS
    packed = jnp.where(
        term == 0, high, jnp.where(term == 1, mid, jnp.where(term == 2, low, 0.0))
    )
    out_ref[0, :, half:] = packed.astype(jnp.bfloat16)
    for idx in range(1, out_ref.shape[0]):
        out_ref[idx] = out_ref[0]


def row_copy(w_ref, start, out_ref, sem):
    depth = out_ref.shape[0]
    start = pl.multiple_of(start, depth)
    return pltpu.make_async_copy(w_ref.at[pl.ds(start, depth), :], out_ref, sem)


def add_rows(hid_ref, offset, w_ref, out_ref, buf_ref, sem, start):
    chunks, depth, _ = buf_ref.shape

    def copy(idx):
        return row_copy(w_ref, start + idx * depth, buf_ref.at[idx], sem.at[idx])

    lax.fori_loop(0, chunks, lambda idx, _: copy(idx).start(), None)

    def step(idx, _):
        copy(idx).wait()
        at = pl.ds(pl.multiple_of(offset + idx * depth, depth), depth)
        out_ref[...] += jnp.dot(hid_ref[:, at], buf_ref[idx], preferred_element_type=jnp.float32)

    return lambda: lax.fori_loop(0, chunks, step, None)


def hidden_kernel(
    where_ref,
    own_ref,
    other_ref,
    gain_ref,
    wg_ref,
    wu_ref,
    wd_ref,
    out_ref,
    down_ref,
    x_ref,
    gate_ref,
    buf_ref,
    sem,
    down_sem,
):
    slots, _, tile = buf_ref.shape
    half = own_ref.shape[2] - LANES
    chunks = out_ref.shape[1] // tile
    down = row_copy(wd_ref, where_ref[0] * out_ref.shape[1], down_ref, down_sem)

    def columns(idx):
        return pl.ds(pl.multiple_of(idx * tile, tile), tile)

    def up_copy(idx):
        slot = lax.rem(idx, slots)
        return pltpu.make_async_copy(wu_ref.at[:, columns(idx)], buf_ref.at[slot], sem.at[slot])

    lax.fori_loop(0, slots, lambda idx, _: up_copy(idx).start(), None)
    is_first = where_ref[0] == 0
    own = flat(own_ref)[:, :half]
    other = flat(other_ref)[:, :half]
    square = jnp.sum(own * own, axis=-1, keepdims=True)
    square = square + jnp.sum(other * other, axis=-1, keepdims=True)
    inv_rms = lax.rsqrt(square / (2 * half) + EPS)
    left = jnp.where(is_first, own, other)
    right = jnp.where(is_first, other, own)
    gain = gain_ref[...].astype(jnp.float32).reshape(1, -1)
    x_ref[:, :half] = (left * inv_rms * gain[:, :half]).astype(jnp.bfloat16)
    x_ref[:, half:] = (right * inv_rms * gain[:, half:]).astype(jnp.bfloat16)

    def gate_step(idx, _):
        at = columns(idx)
        gate = jnp.dot(x_ref[...], wg_ref[:, at], preferred_element_type=jnp.float32)
        gate_ref[:, at] = gate / (1.0 + jnp.exp(-gate))

    lax.fori_loop(0, chunks, gate_step, None)

    def up_step(idx, _):
        up_copy(idx).wait()
        up = jnp.dot(
            x_ref[...], buf_ref[lax.rem(idx, slots)], preferred_element_type=jnp.float32
        )
        at = columns(idx)
        out_ref[:, at] = (gate_ref[:, at] * up).astype(jnp.bfloat16)

        @pl.when(idx + slots < chunks)
        def _():
            up_copy(idx + slots).start()

        @pl.when(idx + slots == chunks)
        def _():
            down.start()

    lax.fori_loop(0, chunks, up_step, None)
    down.wait()


def down_own_kernel(where_ref, hid_ref, held_ref, w_ref, out_ref, buf_ref, sem):
    held = held_ref.shape[0]
    start = where_ref[0] * hid_ref.shape[1] + held
    rest = add_rows(hid_ref, held, w_ref, out_ref, buf_ref, sem, start)
    tile = out_ref.shape[1] // DOWN_TILES

    def step(idx, _):
        at = pl.ds(pl.multiple_of(idx * tile, tile), tile)
        out_ref[:, at] = jnp.dot(
            hid_ref[:, :held], held_ref[:, at], preferred_element_type=jnp.float32
        )

    lax.fori_loop(0, DOWN_TILES, step, None)
    rest()


def down_other_kernel(
    where_ref, hid_ref, part_ref, extra_ref, w_ref, out_ref, total_ref, buf_ref, sem
):
    start = (1 - where_ref[0]) * hid_ref.shape[1]
    rest = add_rows(hid_ref, 0, w_ref, total_ref, buf_ref, sem, start)
    total_ref[...] = part_ref[...]
    rest()
    total = total_ref[...]
    extra = flat(extra_ref)[:, -LANES:]
    lane = lax.broadcasted_iota(jnp.int32, extra.shape, 1)
    mine = (lane % EXPERTS == where_ref[1]) & (lane < 3 * EXPERTS)
    weight = jnp.sum(jnp.where(mine, extra, 0.0), axis=-1, keepdims=True)
    total = total * weight
    blocks, tok, _ = out_ref.shape
    for idx in range(blocks):
        out_ref[idx] = total[idx * tok : (idx + 1) * tok].astype(jnp.bfloat16)


def final_kernel(carried_ref, received_ref, out_ref):
    micro, dev, half = out_ref.shape
    moe = received_ref[0].astype(jnp.float32)
    for idx in range(1, received_ref.shape[0]):
        moe = moe + received_ref[idx].astype(jnp.float32)
    total = carried_ref[0, :, :half].astype(jnp.float32) + moe
    for idx in range(micro):
        out_ref[idx] = total[idx * dev : (idx + 1) * dev].astype(jnp.bfloat16)


SMEM = pl.BlockSpec(memory_space=pltpu.SMEM)
VMEM = pl.BlockSpec(memory_space=pltpu.VMEM)
ANY = pl.BlockSpec(memory_space=pl.ANY)


def call(kernel, out_shape, in_specs, args, scratch=(), limit=SMALL):
    return pl.pallas_call(
        kernel,
        out_shape=out_shape,
        in_specs=in_specs,
        out_specs=[VMEM] * len(out_shape) if isinstance(out_shape, tuple) else VMEM,
        scratch_shapes=scratch,
        compiler_params=pltpu.CompilerParams(vmem_limit_bytes=limit),
    )(*args)


def in_vmem(array):
    return pltpu.with_memory_space_constraint(array, pltpu.VMEM)


def in_hbm(array):
    return pltpu.with_memory_space_constraint(array, pltpu.HBM)


def swap(array, axis, mask):
    size = lax.axis_size(axis)
    return lax.ppermute(array, axis, [(i, i ^ mask) for i in range(size)])


def per_device(
    residual,
    queries,
    key_cache,
    value_cache,
    page_table,
    lengths,
    routes,
    gate_fixed,
    norm_gain,
    w_gate,
    w_up,
    w_down,
):
    micro_count, tok_dev, half = residual.shape
    side_size = lax.axis_size("side")
    tok = micro_count * tok_dev
    rows = tok * side_size
    span = side_size // EXPERTS
    small = SMALL + 64 * rows * half
    width = w_gate.shape[1]
    where = jnp.stack([lax.axis_index("tp"), lax.axis_index("side") // span]).astype(jnp.int32)
    small_args = (page_table, lengths, routes, gate_fixed)
    large_args = (residual, queries, key_cache, value_cache)
    local = call(
        attend_kernel,
        jax.ShapeDtypeStruct((side_size, tok, half + LANES), jnp.bfloat16),
        [SMEM] + [ANY] * 10,
        (where, *[in_hbm(arg) for arg in (*small_args, *large_args, w_gate, w_up)]),
        (
            *[pltpu.SMEM(arg.shape, arg.dtype) for arg in small_args],
            *[pltpu.VMEM(arg.shape, arg.dtype) for arg in large_args],
            pltpu.SemaphoreType.DMA((8,)),
        ),
        small,
    )
    gathered = lax.all_to_all(local, "side", split_axis=0, concat_axis=0, tiled=True)
    other = swap(gathered, "tp", 1)
    tile = math.gcd(width, 512)
    slots = min(width // tile, 6)
    early = width // 2
    depth = math.gcd(width - early, 512)
    held = pltpu.VMEM((early, half), w_down.dtype)

    def stream(count):
        return (
            pltpu.VMEM((count // depth, depth, half), w_down.dtype),
            pltpu.SemaphoreType.DMA((count // depth,)),
        )

    hidden, down_own = call(
        hidden_kernel,
        (pltpu.VMEM((rows, width), jnp.bfloat16), held),
        [SMEM] + [VMEM] * 4 + [ANY] * 2,
        (where, in_vmem(gathered), in_vmem(other), norm_gain, in_vmem(w_gate), in_hbm(w_up), in_hbm(w_down)),
        (
            pltpu.VMEM((rows, 2 * half), jnp.bfloat16),
            pltpu.VMEM((rows, width), jnp.float32),
            pltpu.VMEM((slots, 2 * half, tile), jnp.bfloat16),
            pltpu.SemaphoreType.DMA((slots,)),
            pltpu.SemaphoreType.DMA,
        ),
        SMALL + rows * half * 24 + slots * half * tile * 4,
    )
    hidden_other = swap(hidden, "tp", 1)
    part = call(
        down_own_kernel,
        jax.ShapeDtypeStruct((rows, half), jnp.float32),
        [SMEM] + [VMEM] * 2 + [ANY],
        (where, in_vmem(hidden), in_vmem(down_own), in_hbm(w_down)),
        stream(width - early),
        small + width * half * 2,
    )
    sent = call(
        down_other_kernel,
        jax.ShapeDtypeStruct((side_size, tok, half), jnp.bfloat16),
        [SMEM] + [VMEM] * 3 + [ANY],
        (where, hidden_other, part, gathered, in_hbm(w_down)),
        (pltpu.VMEM((rows, half), jnp.float32), *stream(width)),
        small + width * half * 2,
    )
    received = lax.all_to_all(sent, "side", split_axis=0, concat_axis=0, tiled=True)
    return call(
        final_kernel,
        jax.ShapeDtypeStruct(residual.shape, residual.dtype),
        [VMEM] * 2,
        (local, received),
        limit=small,
    )


def solution(mesh):
    in_specs = (
        P(None, ("groups", "side"), "tp"),
        P(None, ("groups", "side"), "tp"),
        P(("groups", "side"), None, "tp"),
        P(("groups", "side"), None, "tp"),
        P(None, ("groups", "side"), None),
        P(None, ("groups", "side")),
        P(None, ("groups", "side"), None),
        P(None, ("groups", "side")),
        P(),
        P(None, ("side", "tp")),
        P(None, ("side", "tp")),
        P("side", "tp"),
    )
    out_specs = P(None, ("groups", "side"), "tp")
    return jax.shard_map(
        per_device, mesh=mesh, in_specs=in_specs, out_specs=out_specs, check_vma=False
    )
```

```python
import functools
import math

import jax
import jax.numpy as jnp
from jax import lax
from jax.experimental import pallas as pl
from jax.experimental.pallas import tpu as pltpu
from jax.sharding import PartitionSpec as P

HEAD_DIM = 128
EXPERTS = 4
EPS = 1e-05
GATE_ONE = 65536.0
LANES = 128
SMALL = 2 << 20


def by_row(shape, scalars):
    token = lax.broadcasted_iota(jnp.int32, shape, 0) % len(scalars)
    out = jnp.full(shape, scalars[0])
    for idx in range(1, len(scalars)):
        out = jnp.where(token == idx, scalars[idx], out)
    return out


def flat(ref):
    return jnp.concatenate([ref[idx].astype(jnp.float32) for idx in range(ref.shape[0])], axis=0)


def attend_kernel(*refs):
    count = 8
    _where, sources, buffers = refs[0], refs[1 : 1 + count], refs[-1 - count : -1]
    out_ref, sem = refs[-2 - count], refs[-1]
    copies = [
        pltpu.make_async_copy(source, buffer, sem.at[idx])
        for idx, (source, buffer) in enumerate(zip(sources, buffers))
    ]
    for copy in copies:
        copy.start()
    for copy in copies:
        copy.wait()
    pages_ref, len_ref, routes_ref, gate_ref, res_ref, q_ref, k_ref, v_ref = buffers
    micro, dev, half = res_ref.shape
    tok = micro * dev
    pages, page, kv_width = k_ref.shape
    kv_local = kv_width // HEAD_DIM
    group = half // kv_width
    inv_root = 1.0 / math.sqrt(HEAD_DIM)
    keys = k_ref[...].reshape(pages * page, kv_width)
    values = v_ref[...].reshape(pages * page, kv_width)
    shape = (group * tok, pages * page)
    slot = lax.broadcasted_iota(jnp.int32, shape, 1)
    slot_page, offset = slot // page, slot % page
    position = jnp.full(shape, 1 << 20, jnp.int32)
    for nth in range(pages_ref.shape[2]):
        owner = by_row(shape, [pages_ref[t // dev, t % dev, nth] for t in range(tok)])
        position = jnp.where(slot_page == owner, offset + nth * page, position)
    live = position < by_row(shape, [len_ref[t // dev, t % dev] for t in range(tok)])
    queries = flat(q_ref)
    residual = flat(res_ref)
    for head in range(kv_local):
        cols = slice(head * HEAD_DIM, (head + 1) * HEAD_DIM)
        first = head * group
        rows = jnp.concatenate(
            [
                queries[:, (first + g) * HEAD_DIM : (first + g + 1) * HEAD_DIM]
                for g in range(group)
            ],
            axis=0,
        ).astype(jnp.bfloat16)
        scores = lax.dot_general(
            rows, keys[:, cols], (((1,), (1,)), ((), ())), preferred_element_type=jnp.float32
        )
        scores = jnp.where(live, scores * inv_root, -1e30)
        row_max = jnp.max(scores, axis=-1, keepdims=True)
        unnorm = jnp.where(live, jnp.exp(scores - row_max), 0.0)
        denom = jnp.sum(unnorm, axis=-1, keepdims=True)
        blended = (
            jnp.dot(
                unnorm.astype(jnp.bfloat16), values[:, cols], preferred_element_type=jnp.float32
            )
            / denom
        )
        for g in range(group):
            at = slice((first + g) * HEAD_DIM, (first + g + 1) * HEAD_DIM)
            carried = residual[:, at] + blended[g * tok : (g + 1) * tok]
            out_ref[0, :, at] = carried.astype(jnp.bfloat16)
    lane = lax.broadcasted_iota(jnp.int32, (tok, LANES), 1)
    expert = lane % EXPERTS
    fixed = by_row((tok, LANES), [gate_ref[t // dev, t % dev] for t in range(tok)])
    one = by_row((tok, LANES), [routes_ref[t // dev, t % dev, 0] for t in range(tok)])
    two = by_row((tok, LANES), [routes_ref[t // dev, t % dev, 1] for t in range(tok)])
    fixed = fixed.astype(jnp.float32)
    weight = jnp.where(expert == one, fixed / GATE_ONE, 0.0) + jnp.where(
        expert == two, (GATE_ONE - fixed) / GATE_ONE, 0.0
    )
    high = weight.astype(jnp.bfloat16).astype(jnp.float32)
    mid = (weight - high).astype(jnp.bfloat16).astype(jnp.float32)
    low = weight - high - mid
    term = lane // EXPERTS
    packed = jnp.where(
        term == 0, high, jnp.where(term == 1, mid, jnp.where(term == 2, low, 0.0))
    )
    out_ref[0, :, half:] = packed.astype(jnp.bfloat16)
    for idx in range(1, out_ref.shape[0]):
        out_ref[idx] = out_ref[0]


def row_copy(w_ref, start, out_ref, sem):
    depth = out_ref.shape[0]
    start = pl.multiple_of(start, depth)
    return pltpu.make_async_copy(w_ref.at[pl.ds(start, depth), :], out_ref, sem)


def add_rows(hid_ref, offset, w_ref, out_ref, buf_ref, sem, start):
    chunks, depth, _ = buf_ref.shape

    def copy(idx):
        return row_copy(w_ref, start + idx * depth, buf_ref.at[idx], sem.at[idx])

    lax.fori_loop(0, chunks, lambda idx, _: copy(idx).start(), None)

    def step(idx, _):
        copy(idx).wait()
        at = pl.ds(pl.multiple_of(offset + idx * depth, depth), depth)
        out_ref[...] += jnp.dot(hid_ref[:, at], buf_ref[idx], preferred_element_type=jnp.float32)

    return lambda: lax.fori_loop(0, chunks, step, None)


def hidden_kernel(
    where_ref,
    own_ref,
    other_ref,
    gain_ref,
    wg_ref,
    wu_ref,
    wd_ref,
    out_ref,
    part_ref,
    down_ref,
    x_ref,
    gate_ref,
    buf_ref,
    own_buf_ref,
    sem,
    own_sem,
    down_sem,
):
    slots, _, tile = buf_ref.shape
    half = own_ref.shape[2] - LANES
    chunks = out_ref.shape[1] // tile
    own_chunks, depth, _ = own_buf_ref.shape
    own_ahead = own_chunks // 2
    own_start = where_ref[0] * out_ref.shape[1]
    other_start = (1 - where_ref[0]) * out_ref.shape[1]
    down = row_copy(wd_ref, other_start, down_ref, down_sem)

    def own_copy(idx):
        return row_copy(wd_ref, own_start + idx * depth, own_buf_ref.at[idx], own_sem.at[idx])

    def columns(idx):
        return pl.ds(pl.multiple_of(idx * tile, tile), tile)

    def up_copy(idx):
        slot = lax.rem(idx, slots)
        return pltpu.make_async_copy(wu_ref.at[:, columns(idx)], buf_ref.at[slot], sem.at[slot])

    lax.fori_loop(0, slots, lambda idx, _: up_copy(idx).start(), None)
    lax.fori_loop(0, own_ahead, lambda idx, _: own_copy(idx).start(), None)
    is_first = where_ref[0] == 0
    own = flat(own_ref)[:, :half]
    other = flat(other_ref)[:, :half]
    square = jnp.sum(own * own, axis=-1, keepdims=True)
    square = square + jnp.sum(other * other, axis=-1, keepdims=True)
    inv_rms = lax.rsqrt(square / (2 * half) + EPS)
    left = jnp.where(is_first, own, other)
    right = jnp.where(is_first, other, own)
    gain = gain_ref[...].astype(jnp.float32).reshape(1, -1)
    x_ref[:, :half] = (left * inv_rms * gain[:, :half]).astype(jnp.bfloat16)
    x_ref[:, half:] = (right * inv_rms * gain[:, half:]).astype(jnp.bfloat16)

    def gate_step(idx, _):
        at = columns(idx)
        gate = jnp.dot(x_ref[...], wg_ref[:, at], preferred_element_type=jnp.float32)
        gate_ref[:, at] = gate / (1.0 + jnp.exp(-gate))

    lax.fori_loop(0, chunks, gate_step, None)

    def up_step(idx, _):
        up_copy(idx).wait()
        up = jnp.dot(
            x_ref[...], buf_ref[lax.rem(idx, slots)], preferred_element_type=jnp.float32
        )
        at = columns(idx)
        out_ref[:, at] = (gate_ref[:, at] * up).astype(jnp.bfloat16)

        @pl.when(idx + slots < chunks)
        def _():
            up_copy(idx + slots).start()

        @pl.when(idx + slots == chunks)
        def _():
            lax.fori_loop(own_ahead, own_chunks, lambda nth, _: own_copy(nth).start(), None)
            down.start()

    lax.fori_loop(0, chunks, up_step, None)
    part_ref[...] = jnp.zeros_like(part_ref)

    def own_step(idx, _):
        own_copy(idx).wait()
        at = pl.ds(pl.multiple_of(idx * depth, depth), depth)
        part_ref[...] += jnp.dot(
            out_ref[:, at], own_buf_ref[idx], preferred_element_type=jnp.float32
        )

    lax.fori_loop(0, own_chunks, own_step, None)
    down.wait()


def down_other_kernel(
    where_ref, hid_ref, part_ref, extra_ref, held_ref, w_ref, out_ref, total_ref, buf_ref, sem
):
    held, depth = held_ref.shape[0], buf_ref.shape[1]
    start = (1 - where_ref[0]) * hid_ref.shape[1] + held
    rest = add_rows(hid_ref, held, w_ref, total_ref, buf_ref, sem, start)
    total_ref[...] = part_ref[...]

    def step(idx, _):
        at = pl.ds(pl.multiple_of(idx * depth, depth), depth)
        total_ref[...] += jnp.dot(hid_ref[:, at], held_ref[at, :], preferred_element_type=jnp.float32)

    lax.fori_loop(0, held // depth, step, None)
    rest()
    total = total_ref[...]
    extra = flat(extra_ref)[:, -LANES:]
    lane = lax.broadcasted_iota(jnp.int32, extra.shape, 1)
    mine = (lane % EXPERTS == where_ref[1]) & (lane < 3 * EXPERTS)
    weight = jnp.sum(jnp.where(mine, extra, 0.0), axis=-1, keepdims=True)
    total = total * weight
    blocks, tok, _ = out_ref.shape
    for idx in range(blocks):
        out_ref[idx] = total[idx * tok : (idx + 1) * tok].astype(jnp.bfloat16)


def final_kernel(carried_ref, received_ref, out_ref):
    micro, dev, half = out_ref.shape
    moe = received_ref[0].astype(jnp.float32)
    for idx in range(1, received_ref.shape[0]):
        moe = moe + received_ref[idx].astype(jnp.float32)
    total = carried_ref[0, :, :half].astype(jnp.float32) + moe
    for idx in range(micro):
        out_ref[idx] = total[idx * dev : (idx + 1) * dev].astype(jnp.bfloat16)


SMEM = pl.BlockSpec(memory_space=pltpu.SMEM)
VMEM = pl.BlockSpec(memory_space=pltpu.VMEM)
ANY = pl.BlockSpec(memory_space=pl.ANY)


def call(kernel, out_shape, in_specs, args, scratch=(), limit=SMALL):
    return pl.pallas_call(
        kernel,
        out_shape=out_shape,
        in_specs=in_specs,
        out_specs=[VMEM] * len(out_shape) if isinstance(out_shape, tuple) else VMEM,
        scratch_shapes=scratch,
        compiler_params=pltpu.CompilerParams(vmem_limit_bytes=limit),
    )(*args)


def in_vmem(array):
    return pltpu.with_memory_space_constraint(array, pltpu.VMEM)


def in_hbm(array):
    return pltpu.with_memory_space_constraint(array, pltpu.HBM)


def swap(array, axis, mask):
    size = lax.axis_size(axis)
    return lax.ppermute(array, axis, [(i, i ^ mask) for i in range(size)])


def per_device(
    residual,
    queries,
    key_cache,
    value_cache,
    page_table,
    lengths,
    routes,
    gate_fixed,
    norm_gain,
    w_gate,
    w_up,
    w_down,
):
    micro_count, tok_dev, half = residual.shape
    side_size = lax.axis_size("side")
    tok = micro_count * tok_dev
    rows = tok * side_size
    span = side_size // EXPERTS
    small = SMALL + 64 * rows * half
    width = w_gate.shape[1]
    where = jnp.stack([lax.axis_index("tp"), lax.axis_index("side") // span]).astype(jnp.int32)
    small_args = (page_table, lengths, routes, gate_fixed)
    large_args = (residual, queries, key_cache, value_cache)
    local = call(
        attend_kernel,
        jax.ShapeDtypeStruct((side_size, tok, half + LANES), jnp.bfloat16),
        [SMEM] + [ANY] * 10,
        (where, *[in_hbm(arg) for arg in (*small_args, *large_args, w_gate, w_up)]),
        (
            *[pltpu.SMEM(arg.shape, arg.dtype) for arg in small_args],
            *[pltpu.VMEM(arg.shape, arg.dtype) for arg in large_args],
            pltpu.SemaphoreType.DMA((8,)),
        ),
        small,
    )
    gathered = lax.all_to_all(local, "side", split_axis=0, concat_axis=0, tiled=True)
    other = swap(gathered, "tp", 1)
    tile = math.gcd(width, 512)
    slots = min(width // tile, 4)
    early = width * 1 // 2
    depth = math.gcd(width - early, early, 512)
    held = pltpu.VMEM((early, half), w_down.dtype)

    def stream(count):
        return (
            pltpu.VMEM((count // depth, depth, half), w_down.dtype),
            pltpu.SemaphoreType.DMA((count // depth,)),
        )

    hidden, part, down_other = call(
        hidden_kernel,
        (
            pltpu.VMEM((rows, width), jnp.bfloat16),
            pltpu.VMEM((rows, half), jnp.float32),
            held,
        ),
        [SMEM] + [VMEM] * 4 + [ANY] * 2,
        (where, in_vmem(gathered), in_vmem(other), norm_gain, in_vmem(w_gate), in_hbm(w_up), in_hbm(w_down)),
        (
            pltpu.VMEM((rows, 2 * half), jnp.bfloat16),
            pltpu.VMEM((rows, width), jnp.float32),
            pltpu.VMEM((slots, 2 * half, tile), jnp.bfloat16),
            pltpu.VMEM((width // depth, depth, half), w_down.dtype),
            pltpu.SemaphoreType.DMA((slots,)),
            pltpu.SemaphoreType.DMA((width // depth,)),
            pltpu.SemaphoreType.DMA,
        ),
        SMALL + rows * half * 24 + slots * half * tile * 4 + width * half * 2,
    )
    hidden_other = swap(hidden, "tp", 1)
    sent = call(
        down_other_kernel,
        jax.ShapeDtypeStruct((side_size, tok, half), jnp.bfloat16),
        [SMEM] + [VMEM] * 4 + [ANY],
        (where, hidden_other, in_vmem(part), gathered, in_vmem(down_other), in_hbm(w_down)),
        (pltpu.VMEM((rows, half), jnp.float32), *stream(width - early)),
        small + width * half * 2,
    )
    received = lax.all_to_all(sent, "side", split_axis=0, concat_axis=0, tiled=True)
    return call(
        final_kernel,
        jax.ShapeDtypeStruct(residual.shape, residual.dtype),
        [VMEM] * 2,
        (local, received),
        limit=small,
    )


def solution(mesh):
    in_specs = (
        P(None, ("groups", "side"), "tp"),
        P(None, ("groups", "side"), "tp"),
        P(("groups", "side"), None, "tp"),
        P(("groups", "side"), None, "tp"),
        P(None, ("groups", "side"), None),
        P(None, ("groups", "side")),
        P(None, ("groups", "side"), None),
        P(None, ("groups", "side")),
        P(),
        P(None, ("side", "tp")),
        P(None, ("side", "tp")),
        P("side", "tp"),
    )
    out_specs = P(None, ("groups", "side"), "tp")
    return jax.shard_map(
        per_device, mesh=mesh, in_specs=in_specs, out_specs=out_specs, check_vma=False
    )
```

```python
import functools
import math

import jax
import jax.numpy as jnp
from jax import lax
from jax.experimental import pallas as pl
from jax.experimental.pallas import tpu as pltpu
from jax.sharding import PartitionSpec as P

HEAD_DIM = 128
EXPERTS = 4
EPS = 1e-05
GATE_ONE = 65536.0
LANES = 128
SMALL = 2 << 20


def by_row(shape, scalars):
    token = lax.broadcasted_iota(jnp.int32, shape, 0) % len(scalars)
    out = jnp.full(shape, scalars[0])
    for idx in range(1, len(scalars)):
        out = jnp.where(token == idx, scalars[idx], out)
    return out


def flat(ref):
    return jnp.concatenate([ref[idx].astype(jnp.float32) for idx in range(ref.shape[0])], axis=0)


def attend_kernel(*refs):
    count = 8
    _where, sources, buffers = refs[0], refs[1 : 1 + count], refs[-1 - count : -1]
    out_ref, sem = refs[-2 - count], refs[-1]
    copies = [
        pltpu.make_async_copy(source, buffer, sem.at[idx])
        for idx, (source, buffer) in enumerate(zip(sources, buffers))
    ]
    for copy in copies:
        copy.start()
    for copy in copies:
        copy.wait()
    pages_ref, len_ref, routes_ref, gate_ref, res_ref, q_ref, k_ref, v_ref = buffers
    micro, dev, half = res_ref.shape
    tok = micro * dev
    pages, page, kv_width = k_ref.shape
    kv_local = kv_width // HEAD_DIM
    group = half // kv_width
    inv_root = 1.0 / math.sqrt(HEAD_DIM)
    keys = k_ref[...].reshape(pages * page, kv_width)
    values = v_ref[...].reshape(pages * page, kv_width)
    shape = (group * tok, pages * page)
    slot = lax.broadcasted_iota(jnp.int32, shape, 1)
    slot_page, offset = slot // page, slot % page
    position = jnp.full(shape, 1 << 20, jnp.int32)
    for nth in range(pages_ref.shape[2]):
        owner = by_row(shape, [pages_ref[t // dev, t % dev, nth] for t in range(tok)])
        position = jnp.where(slot_page == owner, offset + nth * page, position)
    live = position < by_row(shape, [len_ref[t // dev, t % dev] for t in range(tok)])
    queries = flat(q_ref)
    residual = flat(res_ref)
    for head in range(kv_local):
        cols = slice(head * HEAD_DIM, (head + 1) * HEAD_DIM)
        first = head * group
        rows = jnp.concatenate(
            [
                queries[:, (first + g) * HEAD_DIM : (first + g + 1) * HEAD_DIM]
                for g in range(group)
            ],
            axis=0,
        ).astype(jnp.bfloat16)
        scores = lax.dot_general(
            rows, keys[:, cols], (((1,), (1,)), ((), ())), preferred_element_type=jnp.float32
        )
        scores = jnp.where(live, scores * inv_root, -1e30)
        row_max = jnp.max(scores, axis=-1, keepdims=True)
        unnorm = jnp.where(live, jnp.exp(scores - row_max), 0.0)
        denom = jnp.sum(unnorm, axis=-1, keepdims=True)
        blended = (
            jnp.dot(
                unnorm.astype(jnp.bfloat16), values[:, cols], preferred_element_type=jnp.float32
            )
            / denom
        )
        for g in range(group):
            at = slice((first + g) * HEAD_DIM, (first + g + 1) * HEAD_DIM)
            carried = residual[:, at] + blended[g * tok : (g + 1) * tok]
            out_ref[0, :, at] = carried.astype(jnp.bfloat16)
    lane = lax.broadcasted_iota(jnp.int32, (tok, LANES), 1)
    expert = lane % EXPERTS
    fixed = by_row((tok, LANES), [gate_ref[t // dev, t % dev] for t in range(tok)])
    one = by_row((tok, LANES), [routes_ref[t // dev, t % dev, 0] for t in range(tok)])
    two = by_row((tok, LANES), [routes_ref[t // dev, t % dev, 1] for t in range(tok)])
    fixed = fixed.astype(jnp.float32)
    weight = jnp.where(expert == one, fixed / GATE_ONE, 0.0) + jnp.where(
        expert == two, (GATE_ONE - fixed) / GATE_ONE, 0.0
    )
    high = weight.astype(jnp.bfloat16).astype(jnp.float32)
    mid = (weight - high).astype(jnp.bfloat16).astype(jnp.float32)
    low = weight - high - mid
    term = lane // EXPERTS
    packed = jnp.where(
        term == 0, high, jnp.where(term == 1, mid, jnp.where(term == 2, low, 0.0))
    )
    out_ref[0, :, half:] = packed.astype(jnp.bfloat16)
    for idx in range(1, out_ref.shape[0]):
        out_ref[idx] = out_ref[0]


def row_copy(w_ref, start, out_ref, sem):
    depth = out_ref.shape[0]
    start = pl.multiple_of(start, math.gcd(depth, 512))
    return pltpu.make_async_copy(w_ref.at[pl.ds(start, depth), :], out_ref, sem)


def add_rows(hid_ref, offset, w_ref, out_ref, buf_ref, sem, start):
    chunks, depth, _ = buf_ref.shape

    def copy(idx):
        return row_copy(w_ref, start + idx * depth, buf_ref.at[idx], sem.at[idx])

    lax.fori_loop(0, chunks, lambda idx, _: copy(idx).start(), None)

    def step(idx, _):
        copy(idx).wait()
        at = pl.ds(pl.multiple_of(offset + idx * depth, depth), depth)
        out_ref[...] += jnp.dot(hid_ref[:, at], buf_ref[idx], preferred_element_type=jnp.float32)

    return lambda: lax.fori_loop(0, chunks, step, None)


def hidden_kernel(
    where_ref,
    own_ref,
    other_ref,
    gain_ref,
    wg_ref,
    wu_ref,
    wd_ref,
    out_ref,
    part_ref,
    down_ref,
    x_ref,
    gate_ref,
    buf_ref,
    own_buf_ref,
    sem,
    own_sem,
    down_sem,
):
    slots, _, tile = buf_ref.shape
    half = own_ref.shape[2] - LANES
    chunks = out_ref.shape[1] // tile
    own_chunks, depth, _ = own_buf_ref.shape
    own_ahead = own_chunks // 2
    own_start = where_ref[0] * out_ref.shape[1]
    other_start = (1 - where_ref[0]) * out_ref.shape[1]
    down = row_copy(wd_ref, other_start, down_ref, down_sem)

    def own_copy(idx):
        return row_copy(wd_ref, own_start + idx * depth, own_buf_ref.at[idx], own_sem.at[idx])

    def columns(idx):
        return pl.ds(pl.multiple_of(idx * tile, tile), tile)

    def up_copy(idx):
        slot = lax.rem(idx, slots)
        return pltpu.make_async_copy(wu_ref.at[:, columns(idx)], buf_ref.at[slot], sem.at[slot])

    lax.fori_loop(0, slots, lambda idx, _: up_copy(idx).start(), None)
    lax.fori_loop(0, own_ahead, lambda idx, _: own_copy(idx).start(), None)
    is_first = where_ref[0] == 0
    own = flat(own_ref)[:, :half]
    other = flat(other_ref)[:, :half]
    square = jnp.sum(own * own, axis=-1, keepdims=True)
    square = square + jnp.sum(other * other, axis=-1, keepdims=True)
    inv_rms = lax.rsqrt(square / (2 * half) + EPS)
    left = jnp.where(is_first, own, other)
    right = jnp.where(is_first, other, own)
    gain = gain_ref[...].astype(jnp.float32).reshape(1, -1)
    x_ref[:, :half] = (left * inv_rms * gain[:, :half]).astype(jnp.bfloat16)
    x_ref[:, half:] = (right * inv_rms * gain[:, half:]).astype(jnp.bfloat16)

    wide = math.gcd(out_ref.shape[1], 2048)

    def gate_step(idx, _):
        at = pl.ds(pl.multiple_of(idx * wide, wide), wide)
        gate = jnp.dot(x_ref[...], wg_ref[:, at], preferred_element_type=jnp.float32)
        gate_ref[:, at] = gate / (1.0 + jnp.exp(-gate))

    lax.fori_loop(0, out_ref.shape[1] // wide, gate_step, None)

    def up_step(idx, _):
        up_copy(idx).wait()
        up = jnp.dot(
            x_ref[...], buf_ref[lax.rem(idx, slots)], preferred_element_type=jnp.float32
        )
        at = columns(idx)
        out_ref[:, at] = (gate_ref[:, at] * up).astype(jnp.bfloat16)

        @pl.when(idx + slots < chunks)
        def _():
            up_copy(idx + slots).start()

        @pl.when(idx + slots == chunks)
        def _():
            lax.fori_loop(own_ahead, own_chunks, lambda nth, _: own_copy(nth).start(), None)
            down.start()

    lax.fori_loop(0, chunks, up_step, None)
    part_ref[...] = jnp.zeros_like(part_ref)

    def own_step(idx, _):
        own_copy(idx).wait()
        at = pl.ds(pl.multiple_of(idx * depth, depth), depth)
        part_ref[...] += jnp.dot(
            out_ref[:, at], own_buf_ref[idx], preferred_element_type=jnp.float32
        )

    lax.fori_loop(0, own_chunks, own_step, None)
    down.wait()


def down_other_kernel(
    where_ref, hid_ref, part_ref, extra_ref, held_ref, w_ref, out_ref, total_ref, buf_ref, sem
):
    held, depth = held_ref.shape[0], buf_ref.shape[1]
    start = (1 - where_ref[0]) * hid_ref.shape[1] + held
    rest = add_rows(hid_ref, held, w_ref, total_ref, buf_ref, sem, start)
    total_ref[...] = part_ref[...]

    def step(idx, _):
        at = pl.ds(pl.multiple_of(idx * depth, depth), depth)
        total_ref[...] += jnp.dot(hid_ref[:, at], held_ref[at, :], preferred_element_type=jnp.float32)

    lax.fori_loop(0, held // depth, step, None)
    rest()
    total = total_ref[...]
    extra = flat(extra_ref)[:, -LANES:]
    lane = lax.broadcasted_iota(jnp.int32, extra.shape, 1)
    mine = (lane % EXPERTS == where_ref[1]) & (lane < 3 * EXPERTS)
    weight = jnp.sum(jnp.where(mine, extra, 0.0), axis=-1, keepdims=True)
    total = total * weight
    blocks, tok, _ = out_ref.shape
    for idx in range(blocks):
        out_ref[idx] = total[idx * tok : (idx + 1) * tok].astype(jnp.bfloat16)


def final_kernel(carried_ref, received_ref, out_ref):
    micro, dev, half = out_ref.shape
    moe = received_ref[0].astype(jnp.float32)
    for idx in range(1, received_ref.shape[0]):
        moe = moe + received_ref[idx].astype(jnp.float32)
    total = carried_ref[0, :, :half].astype(jnp.float32) + moe
    for idx in range(micro):
        out_ref[idx] = total[idx * dev : (idx + 1) * dev].astype(jnp.bfloat16)


SMEM = pl.BlockSpec(memory_space=pltpu.SMEM)
VMEM = pl.BlockSpec(memory_space=pltpu.VMEM)
ANY = pl.BlockSpec(memory_space=pl.ANY)


def call(kernel, out_shape, in_specs, args, scratch=(), limit=SMALL):
    return pl.pallas_call(
        kernel,
        out_shape=out_shape,
        in_specs=in_specs,
        out_specs=[VMEM] * len(out_shape) if isinstance(out_shape, tuple) else VMEM,
        scratch_shapes=scratch,
        compiler_params=pltpu.CompilerParams(vmem_limit_bytes=limit),
    )(*args)


def in_vmem(array):
    return pltpu.with_memory_space_constraint(array, pltpu.VMEM)


def in_hbm(array):
    return pltpu.with_memory_space_constraint(array, pltpu.HBM)


def swap(array, axis, mask):
    size = lax.axis_size(axis)
    return lax.ppermute(array, axis, [(i, i ^ mask) for i in range(size)])


def per_device(
    residual,
    queries,
    key_cache,
    value_cache,
    page_table,
    lengths,
    routes,
    gate_fixed,
    norm_gain,
    w_gate,
    w_up,
    w_down,
):
    micro_count, tok_dev, half = residual.shape
    side_size = lax.axis_size("side")
    tok = micro_count * tok_dev
    rows = tok * side_size
    span = side_size // EXPERTS
    small = SMALL + 64 * rows * half
    width = w_gate.shape[1]
    where = jnp.stack([lax.axis_index("tp"), lax.axis_index("side") // span]).astype(jnp.int32)
    small_args = (page_table, lengths, routes, gate_fixed)
    large_args = (residual, queries, key_cache, value_cache)
    local = call(
        attend_kernel,
        jax.ShapeDtypeStruct((side_size, tok, half + LANES), jnp.bfloat16),
        [SMEM] + [ANY] * 10,
        (where, *[in_hbm(arg) for arg in (*small_args, *large_args, w_gate, w_up)]),
        (
            *[pltpu.SMEM(arg.shape, arg.dtype) for arg in small_args],
            *[pltpu.VMEM(arg.shape, arg.dtype) for arg in large_args],
            pltpu.SemaphoreType.DMA((8,)),
        ),
        small,
    )
    gathered = lax.all_to_all(local, "side", split_axis=0, concat_axis=0, tiled=True)
    other = swap(gathered, "tp", 1)
    tile = math.gcd(width, 512)
    slots = min(width // tile, 4)
    early = width * 1 // 2
    depth = math.gcd(width - early, early, 512)
    own_depth = math.gcd(width, 1024)
    held = pltpu.VMEM((early, half), w_down.dtype)

    def stream(count):
        return (
            pltpu.VMEM((count // depth, depth, half), w_down.dtype),
            pltpu.SemaphoreType.DMA((count // depth,)),
        )

    hidden, part, down_other = call(
        hidden_kernel,
        (
            pltpu.VMEM((rows, width), jnp.bfloat16),
            pltpu.VMEM((rows, half), jnp.float32),
            held,
        ),
        [SMEM] + [VMEM] * 4 + [ANY] * 2,
        (where, in_vmem(gathered), in_vmem(other), norm_gain, in_vmem(w_gate), in_hbm(w_up), in_hbm(w_down)),
        (
            pltpu.VMEM((rows, 2 * half), jnp.bfloat16),
            pltpu.VMEM((rows, width), jnp.float32),
            pltpu.VMEM((slots, 2 * half, tile), jnp.bfloat16),
            pltpu.VMEM((width // own_depth, own_depth, half), w_down.dtype),
            pltpu.SemaphoreType.DMA((slots,)),
            pltpu.SemaphoreType.DMA((width // own_depth,)),
            pltpu.SemaphoreType.DMA,
        ),
        SMALL + rows * half * 24 + slots * half * tile * 4 + width * half * 2,
    )
    hidden_other = swap(hidden, "tp", 1)
    sent = call(
        down_other_kernel,
        jax.ShapeDtypeStruct((side_size, tok, half), jnp.bfloat16),
        [SMEM] + [VMEM] * 4 + [ANY],
        (where, hidden_other, in_vmem(part), gathered, in_vmem(down_other), in_hbm(w_down)),
        (pltpu.VMEM((rows, half), jnp.float32), *stream(width - early)),
        small + width * half * 2,
    )
    received = lax.all_to_all(sent, "side", split_axis=0, concat_axis=0, tiled=True)
    return call(
        final_kernel,
        jax.ShapeDtypeStruct(residual.shape, residual.dtype),
        [VMEM] * 2,
        (local, received),
        limit=small,
    )


def solution(mesh):
    in_specs = (
        P(None, ("groups", "side"), "tp"),
        P(None, ("groups", "side"), "tp"),
        P(("groups", "side"), None, "tp"),
        P(("groups", "side"), None, "tp"),
        P(None, ("groups", "side"), None),
        P(None, ("groups", "side")),
        P(None, ("groups", "side"), None),
        P(None, ("groups", "side")),
        P(),
        P(None, ("side", "tp")),
        P(None, ("side", "tp")),
        P("side", "tp"),
    )
    out_specs = P(None, ("groups", "side"), "tp")
    return jax.shard_map(
        per_device, mesh=mesh, in_specs=in_specs, out_specs=out_specs, check_vma=False
    )
```

```python
import functools
import math

import jax
import jax.numpy as jnp
from jax import lax
from jax.experimental import pallas as pl
from jax.experimental.pallas import tpu as pltpu
from jax.sharding import PartitionSpec as P

HEAD_DIM = 128
EXPERTS = 4
EPS = 1e-05
GATE_ONE = 65536.0
LANES = 128
SMALL = 2 << 20


def by_row(shape, scalars):
    token = lax.broadcasted_iota(jnp.int32, shape, 0) % len(scalars)
    out = jnp.full(shape, scalars[0])
    for idx in range(1, len(scalars)):
        out = jnp.where(token == idx, scalars[idx], out)
    return out


def flat(ref):
    return jnp.concatenate([ref[idx].astype(jnp.float32) for idx in range(ref.shape[0])], axis=0)


def attend_kernel(*refs):
    count = 8
    _where, sources, buffers = refs[0], refs[1 : 1 + count], refs[-1 - count : -1]
    out_ref, sem = refs[-2 - count], refs[-1]
    copies = [
        pltpu.make_async_copy(source, buffer, sem.at[idx])
        for idx, (source, buffer) in enumerate(zip(sources, buffers))
    ]
    for copy in copies:
        copy.start()
    for copy in copies:
        copy.wait()
    pages_ref, len_ref, routes_ref, gate_ref, res_ref, q_ref, k_ref, v_ref = buffers
    micro, dev, half = res_ref.shape
    tok = micro * dev
    pages, page, kv_width = k_ref.shape
    kv_local = kv_width // HEAD_DIM
    group = half // kv_width
    inv_root = 1.0 / math.sqrt(HEAD_DIM)
    keys = k_ref[...].reshape(pages * page, kv_width)
    values = v_ref[...].reshape(pages * page, kv_width)
    shape = (group * tok, pages * page)
    slot = lax.broadcasted_iota(jnp.int32, shape, 1)
    slot_page, offset = slot // page, slot % page
    position = jnp.full(shape, 1 << 20, jnp.int32)
    for nth in range(pages_ref.shape[2]):
        owner = by_row(shape, [pages_ref[t // dev, t % dev, nth] for t in range(tok)])
        position = jnp.where(slot_page == owner, offset + nth * page, position)
    live = position < by_row(shape, [len_ref[t // dev, t % dev] for t in range(tok)])
    queries = flat(q_ref)
    residual = flat(res_ref)
    for head in range(kv_local):
        cols = slice(head * HEAD_DIM, (head + 1) * HEAD_DIM)
        first = head * group
        rows = jnp.concatenate(
            [
                queries[:, (first + g) * HEAD_DIM : (first + g + 1) * HEAD_DIM]
                for g in range(group)
            ],
            axis=0,
        ).astype(jnp.bfloat16)
        scores = lax.dot_general(
            rows, keys[:, cols], (((1,), (1,)), ((), ())), preferred_element_type=jnp.float32
        )
        scores = jnp.where(live, scores * inv_root, -1e30)
        row_max = jnp.max(scores, axis=-1, keepdims=True)
        unnorm = jnp.where(live, jnp.exp(scores - row_max), 0.0)
        denom = jnp.sum(unnorm, axis=-1, keepdims=True)
        blended = (
            jnp.dot(
                unnorm.astype(jnp.bfloat16), values[:, cols], preferred_element_type=jnp.float32
            )
            / denom
        )
        for g in range(group):
            at = slice((first + g) * HEAD_DIM, (first + g + 1) * HEAD_DIM)
            carried = residual[:, at] + blended[g * tok : (g + 1) * tok]
            out_ref[0, :, at] = carried.astype(jnp.bfloat16)
    lane = lax.broadcasted_iota(jnp.int32, (tok, LANES), 1)
    expert = lane % EXPERTS
    fixed = by_row((tok, LANES), [gate_ref[t // dev, t % dev] for t in range(tok)])
    one = by_row((tok, LANES), [routes_ref[t // dev, t % dev, 0] for t in range(tok)])
    two = by_row((tok, LANES), [routes_ref[t // dev, t % dev, 1] for t in range(tok)])
    fixed = fixed.astype(jnp.float32)
    weight = jnp.where(expert == one, fixed / GATE_ONE, 0.0) + jnp.where(
        expert == two, (GATE_ONE - fixed) / GATE_ONE, 0.0
    )
    high = weight.astype(jnp.bfloat16).astype(jnp.float32)
    mid = (weight - high).astype(jnp.bfloat16).astype(jnp.float32)
    low = weight - high - mid
    term = lane // EXPERTS
    packed = jnp.where(
        term == 0, high, jnp.where(term == 1, mid, jnp.where(term == 2, low, 0.0))
    )
    out_ref[0, :, half:] = packed.astype(jnp.bfloat16)
    for idx in range(1, out_ref.shape[0]):
        out_ref[idx] = out_ref[0]


def row_copy(w_ref, start, out_ref, sem):
    depth = out_ref.shape[0]
    start = pl.multiple_of(start, math.gcd(depth, 512))
    return pltpu.make_async_copy(w_ref.at[pl.ds(start, depth), :], out_ref, sem)


def add_rows(hid_ref, offset, w_ref, out_ref, buf_ref, sem, start):
    chunks, depth, _ = buf_ref.shape

    def copy(idx):
        return row_copy(w_ref, start + idx * depth, buf_ref.at[idx], sem.at[idx])

    lax.fori_loop(0, chunks, lambda idx, _: copy(idx).start(), None)

    def step(idx, _):
        copy(idx).wait()
        at = pl.ds(pl.multiple_of(offset + idx * depth, depth), depth)
        out_ref[...] += jnp.dot(hid_ref[:, at], buf_ref[idx], preferred_element_type=jnp.float32)

    return lambda: lax.fori_loop(0, chunks, step, None)


def hidden_kernel(
    where_ref,
    own_ref,
    other_ref,
    gain_ref,
    wg_ref,
    wu_ref,
    wd_ref,
    out_ref,
    part_ref,
    down_ref,
    x_ref,
    gate_ref,
    up_ref,
    buf_ref,
    own_buf_ref,
    sem,
    own_sem,
    down_sem,
):
    slots, deep, _ = buf_ref.shape
    half = own_ref.shape[2] - LANES
    chunks = 2 * half // deep
    own_chunks, depth, _ = own_buf_ref.shape
    own_ahead = own_chunks // 2
    own_start = where_ref[0] * out_ref.shape[1]
    other_start = (1 - where_ref[0]) * out_ref.shape[1]
    down = row_copy(wd_ref, other_start, down_ref, down_sem)

    def own_copy(idx):
        return row_copy(wd_ref, own_start + idx * depth, own_buf_ref.at[idx], own_sem.at[idx])

    def lines(idx):
        return pl.ds(pl.multiple_of(idx * deep, deep), deep)

    def up_copy(idx):
        slot = lax.rem(idx, slots)
        return pltpu.make_async_copy(wu_ref.at[lines(idx), :], buf_ref.at[slot], sem.at[slot])

    lax.fori_loop(0, slots, lambda idx, _: up_copy(idx).start(), None)
    lax.fori_loop(0, own_ahead, lambda idx, _: own_copy(idx).start(), None)
    is_first = where_ref[0] == 0
    own = flat(own_ref)[:, :half]
    other = flat(other_ref)[:, :half]
    square = jnp.sum(own * own, axis=-1, keepdims=True)
    square = square + jnp.sum(other * other, axis=-1, keepdims=True)
    inv_rms = lax.rsqrt(square / (2 * half) + EPS)
    left = jnp.where(is_first, own, other)
    right = jnp.where(is_first, other, own)
    gain = gain_ref[...].astype(jnp.float32).reshape(1, -1)
    x_ref[:, :half] = (left * inv_rms * gain[:, :half]).astype(jnp.bfloat16)
    x_ref[:, half:] = (right * inv_rms * gain[:, half:]).astype(jnp.bfloat16)

    wide = math.gcd(out_ref.shape[1], 2048)

    def gate_step(idx, _):
        at = pl.ds(pl.multiple_of(idx * wide, wide), wide)
        gate = jnp.dot(x_ref[...], wg_ref[:, at], preferred_element_type=jnp.float32)
        gate_ref[:, at] = gate / (1.0 + jnp.exp(-gate))

    lax.fori_loop(0, out_ref.shape[1] // wide, gate_step, None)

    up_ref[...] = jnp.zeros_like(up_ref)

    def up_step(idx, _):
        up_copy(idx).wait()
        up_ref[...] += jnp.dot(
            x_ref[:, lines(idx)], buf_ref[lax.rem(idx, slots)], preferred_element_type=jnp.float32
        )

        @pl.when(idx + slots < chunks)
        def _():
            up_copy(idx + slots).start()

        @pl.when(idx + slots == chunks)
        def _():
            lax.fori_loop(own_ahead, own_chunks, lambda nth, _: own_copy(nth).start(), None)
            down.start()

    lax.fori_loop(0, chunks, up_step, None)
    out_ref[...] = (gate_ref[...] * up_ref[...]).astype(jnp.bfloat16)
    part_ref[...] = jnp.zeros_like(part_ref)

    def own_step(idx, _):
        own_copy(idx).wait()
        at = pl.ds(pl.multiple_of(idx * depth, depth), depth)
        part_ref[...] += jnp.dot(
            out_ref[:, at], own_buf_ref[idx], preferred_element_type=jnp.float32
        )

    lax.fori_loop(0, own_chunks, own_step, None)
    down.wait()


def down_other_kernel(
    where_ref, hid_ref, part_ref, extra_ref, held_ref, w_ref, out_ref, total_ref, buf_ref, sem
):
    held, depth = held_ref.shape[0], buf_ref.shape[1]
    start = (1 - where_ref[0]) * hid_ref.shape[1] + held
    rest = add_rows(hid_ref, held, w_ref, total_ref, buf_ref, sem, start)
    total_ref[...] = part_ref[...]

    def step(idx, _):
        at = pl.ds(pl.multiple_of(idx * depth, depth), depth)
        total_ref[...] += jnp.dot(hid_ref[:, at], held_ref[at, :], preferred_element_type=jnp.float32)

    lax.fori_loop(0, held // depth, step, None)
    rest()
    total = total_ref[...]
    extra = flat(extra_ref)[:, -LANES:]
    lane = lax.broadcasted_iota(jnp.int32, extra.shape, 1)
    mine = (lane % EXPERTS == where_ref[1]) & (lane < 3 * EXPERTS)
    weight = jnp.sum(jnp.where(mine, extra, 0.0), axis=-1, keepdims=True)
    total = total * weight
    blocks, tok, _ = out_ref.shape
    for idx in range(blocks):
        out_ref[idx] = total[idx * tok : (idx + 1) * tok].astype(jnp.bfloat16)


def final_kernel(carried_ref, received_ref, out_ref):
    micro, dev, half = out_ref.shape
    moe = received_ref[0].astype(jnp.float32)
    for idx in range(1, received_ref.shape[0]):
        moe = moe + received_ref[idx].astype(jnp.float32)
    total = carried_ref[0, :, :half].astype(jnp.float32) + moe
    for idx in range(micro):
        out_ref[idx] = total[idx * dev : (idx + 1) * dev].astype(jnp.bfloat16)


SMEM = pl.BlockSpec(memory_space=pltpu.SMEM)
VMEM = pl.BlockSpec(memory_space=pltpu.VMEM)
ANY = pl.BlockSpec(memory_space=pl.ANY)


def call(kernel, out_shape, in_specs, args, scratch=(), limit=SMALL):
    return pl.pallas_call(
        kernel,
        out_shape=out_shape,
        in_specs=in_specs,
        out_specs=[VMEM] * len(out_shape) if isinstance(out_shape, tuple) else VMEM,
        scratch_shapes=scratch,
        compiler_params=pltpu.CompilerParams(vmem_limit_bytes=limit),
    )(*args)


def in_vmem(array):
    return pltpu.with_memory_space_constraint(array, pltpu.VMEM)


def in_hbm(array):
    return pltpu.with_memory_space_constraint(array, pltpu.HBM)


def swap(array, axis, mask):
    size = lax.axis_size(axis)
    return lax.ppermute(array, axis, [(i, i ^ mask) for i in range(size)])


def per_device(
    residual,
    queries,
    key_cache,
    value_cache,
    page_table,
    lengths,
    routes,
    gate_fixed,
    norm_gain,
    w_gate,
    w_up,
    w_down,
):
    micro_count, tok_dev, half = residual.shape
    side_size = lax.axis_size("side")
    tok = micro_count * tok_dev
    rows = tok * side_size
    span = side_size // EXPERTS
    small = SMALL + 64 * rows * half
    width = w_gate.shape[1]
    where = jnp.stack([lax.axis_index("tp"), lax.axis_index("side") // span]).astype(jnp.int32)
    small_args = (page_table, lengths, routes, gate_fixed)
    large_args = (residual, queries, key_cache, value_cache)
    local = call(
        attend_kernel,
        jax.ShapeDtypeStruct((side_size, tok, half + LANES), jnp.bfloat16),
        [SMEM] + [ANY] * 10,
        (where, *[in_hbm(arg) for arg in (*small_args, *large_args, w_gate, w_up)]),
        (
            *[pltpu.SMEM(arg.shape, arg.dtype) for arg in small_args],
            *[pltpu.VMEM(arg.shape, arg.dtype) for arg in large_args],
            pltpu.SemaphoreType.DMA((8,)),
        ),
        small,
    )
    gathered = lax.all_to_all(local, "side", split_axis=0, concat_axis=0, tiled=True)
    other = swap(gathered, "tp", 1)
    deep = math.gcd(2 * half, 256)
    slots = 6
    early = width * 1 // 2
    depth = math.gcd(width - early, early, 512)
    own_depth = math.gcd(width, 1024)
    held = pltpu.VMEM((early, half), w_down.dtype)

    def stream(count):
        return (
            pltpu.VMEM((count // depth, depth, half), w_down.dtype),
            pltpu.SemaphoreType.DMA((count // depth,)),
        )

    hidden, part, down_other = call(
        hidden_kernel,
        (
            pltpu.VMEM((rows, width), jnp.bfloat16),
            pltpu.VMEM((rows, half), jnp.float32),
            held,
        ),
        [SMEM] + [VMEM] * 4 + [ANY] * 2,
        (where, in_vmem(gathered), in_vmem(other), norm_gain, in_vmem(w_gate), in_hbm(w_up), in_hbm(w_down)),
        (
            pltpu.VMEM((rows, 2 * half), jnp.bfloat16),
            pltpu.VMEM((rows, width), jnp.float32),
            pltpu.VMEM((rows, width), jnp.float32),
            pltpu.VMEM((slots, deep, width), jnp.bfloat16),
            pltpu.VMEM((width // own_depth, own_depth, half), w_down.dtype),
            pltpu.SemaphoreType.DMA((slots,)),
            pltpu.SemaphoreType.DMA((width // own_depth,)),
            pltpu.SemaphoreType.DMA,
        ),
        SMALL + rows * half * 24 + slots * deep * width * 2 + rows * width * 4 + width * half * 2,
    )
    hidden_other = swap(hidden, "tp", 1)
    sent = call(
        down_other_kernel,
        jax.ShapeDtypeStruct((side_size, tok, half), jnp.bfloat16),
        [SMEM] + [VMEM] * 4 + [ANY],
        (where, hidden_other, in_vmem(part), gathered, in_vmem(down_other), in_hbm(w_down)),
        (pltpu.VMEM((rows, half), jnp.float32), *stream(width - early)),
        small + width * half * 2,
    )
    received = lax.all_to_all(sent, "side", split_axis=0, concat_axis=0, tiled=True)
    return call(
        final_kernel,
        jax.ShapeDtypeStruct(residual.shape, residual.dtype),
        [VMEM] * 2,
        (local, received),
        limit=small,
    )


def solution(mesh):
    in_specs = (
        P(None, ("groups", "side"), "tp"),
        P(None, ("groups", "side"), "tp"),
        P(("groups", "side"), None, "tp"),
        P(("groups", "side"), None, "tp"),
        P(None, ("groups", "side"), None),
        P(None, ("groups", "side")),
        P(None, ("groups", "side"), None),
        P(None, ("groups", "side")),
        P(),
        P(None, ("side", "tp")),
        P(None, ("side", "tp")),
        P("side", "tp"),
    )
    out_specs = P(None, ("groups", "side"), "tp")
    return jax.shard_map(
        per_device, mesh=mesh, in_specs=in_specs, out_specs=out_specs, check_vma=False
    )
```

```python
import functools
import math

import jax
import jax.numpy as jnp
from jax import lax
from jax.experimental import pallas as pl
from jax.experimental.pallas import tpu as pltpu
from jax.sharding import PartitionSpec as P

HEAD_DIM = 128
EXPERTS = 4
EPS = 1e-05
GATE_ONE = 65536.0
LANES = 128
SMALL = 2 << 20


def by_row(shape, scalars):
    token = lax.broadcasted_iota(jnp.int32, shape, 0) % len(scalars)
    out = jnp.full(shape, scalars[0])
    for idx in range(1, len(scalars)):
        out = jnp.where(token == idx, scalars[idx], out)
    return out


def flat(ref):
    return jnp.concatenate([ref[idx].astype(jnp.float32) for idx in range(ref.shape[0])], axis=0)


def attend_kernel(*refs):
    count = 8
    _where, sources, buffers = refs[0], refs[1 : 1 + count], refs[-1 - count : -1]
    out_ref, sem = refs[-2 - count], refs[-1]
    copies = [
        pltpu.make_async_copy(source, buffer, sem.at[idx])
        for idx, (source, buffer) in enumerate(zip(sources, buffers))
    ]
    for copy in copies:
        copy.start()
    for copy in copies:
        copy.wait()
    pages_ref, len_ref, routes_ref, gate_ref, res_ref, q_ref, k_ref, v_ref = buffers
    micro, dev, half = res_ref.shape
    tok = micro * dev
    pages, page, kv_width = k_ref.shape
    kv_local = kv_width // HEAD_DIM
    group = half // kv_width
    inv_root = 1.0 / math.sqrt(HEAD_DIM)
    keys = k_ref[...].reshape(pages * page, kv_width)
    values = v_ref[...].reshape(pages * page, kv_width)
    shape = (group * tok, pages * page)
    slot = lax.broadcasted_iota(jnp.int32, shape, 1)
    slot_page, offset = slot // page, slot % page
    position = jnp.full(shape, 1 << 20, jnp.int32)
    for nth in range(pages_ref.shape[2]):
        owner = by_row(shape, [pages_ref[t // dev, t % dev, nth] for t in range(tok)])
        position = jnp.where(slot_page == owner, offset + nth * page, position)
    live = position < by_row(shape, [len_ref[t // dev, t % dev] for t in range(tok)])
    queries = flat(q_ref)
    residual = flat(res_ref)
    for head in range(kv_local):
        cols = slice(head * HEAD_DIM, (head + 1) * HEAD_DIM)
        first = head * group
        rows = jnp.concatenate(
            [
                queries[:, (first + g) * HEAD_DIM : (first + g + 1) * HEAD_DIM]
                for g in range(group)
            ],
            axis=0,
        ).astype(jnp.bfloat16)
        scores = lax.dot_general(
            rows, keys[:, cols], (((1,), (1,)), ((), ())), preferred_element_type=jnp.float32
        )
        scores = jnp.where(live, scores * inv_root, -1e30)
        row_max = jnp.max(scores, axis=-1, keepdims=True)
        unnorm = jnp.where(live, jnp.exp(scores - row_max), 0.0)
        denom = jnp.sum(unnorm, axis=-1, keepdims=True)
        blended = (
            jnp.dot(
                unnorm.astype(jnp.bfloat16), values[:, cols], preferred_element_type=jnp.float32
            )
            / denom
        )
        for g in range(group):
            at = slice((first + g) * HEAD_DIM, (first + g + 1) * HEAD_DIM)
            carried = residual[:, at] + blended[g * tok : (g + 1) * tok]
            out_ref[0, :, at] = carried.astype(jnp.bfloat16)
    lane = lax.broadcasted_iota(jnp.int32, (tok, LANES), 1)
    expert = lane % EXPERTS
    fixed = by_row((tok, LANES), [gate_ref[t // dev, t % dev] for t in range(tok)])
    one = by_row((tok, LANES), [routes_ref[t // dev, t % dev, 0] for t in range(tok)])
    two = by_row((tok, LANES), [routes_ref[t // dev, t % dev, 1] for t in range(tok)])
    fixed = fixed.astype(jnp.float32)
    weight = jnp.where(expert == one, fixed / GATE_ONE, 0.0) + jnp.where(
        expert == two, (GATE_ONE - fixed) / GATE_ONE, 0.0
    )
    high = weight.astype(jnp.bfloat16).astype(jnp.float32)
    mid = (weight - high).astype(jnp.bfloat16).astype(jnp.float32)
    low = weight - high - mid
    term = lane // EXPERTS
    packed = jnp.where(
        term == 0, high, jnp.where(term == 1, mid, jnp.where(term == 2, low, 0.0))
    )
    out_ref[0, :, half:] = packed.astype(jnp.bfloat16)
    for idx in range(1, out_ref.shape[0]):
        out_ref[idx] = out_ref[0]


def row_copy(w_ref, start, out_ref, sem):
    depth = out_ref.shape[0]
    start = pl.multiple_of(start, math.gcd(depth, 512))
    return pltpu.make_async_copy(w_ref.at[pl.ds(start, depth), :], out_ref, sem)


def add_rows(hid_ref, offset, w_ref, out_ref, buf_ref, sem, start):
    chunks, depth, _ = buf_ref.shape

    def copy(idx):
        return row_copy(w_ref, start + idx * depth, buf_ref.at[idx], sem.at[idx])

    lax.fori_loop(0, chunks, lambda idx, _: copy(idx).start(), None)

    def step(idx, _):
        copy(idx).wait()
        at = pl.ds(pl.multiple_of(offset + idx * depth, depth), depth)
        out_ref[...] += jnp.dot(hid_ref[:, at], buf_ref[idx], preferred_element_type=jnp.float32)

    return lambda: lax.fori_loop(0, chunks, step, None)


def hidden_kernel(
    where_ref,
    own_ref,
    other_ref,
    gain_ref,
    wg_ref,
    wu_ref,
    wd_ref,
    out_ref,
    part_ref,
    down_ref,
    x_ref,
    gate_ref,
    up_ref,
    buf_ref,
    own_buf_ref,
    sem,
    own_sem,
    down_sem,
):
    slots, deep, _ = buf_ref.shape
    half = own_ref.shape[2] - LANES
    chunks = 2 * half // deep
    own_chunks, depth, _ = own_buf_ref.shape
    own_ahead = own_chunks // 2
    own_start = where_ref[0] * out_ref.shape[1]
    other_start = (1 - where_ref[0]) * out_ref.shape[1]
    down = row_copy(wd_ref, other_start, down_ref, down_sem)

    def own_copy(idx):
        return row_copy(wd_ref, own_start + idx * depth, own_buf_ref.at[idx], own_sem.at[idx])

    def lines(idx):
        return pl.ds(pl.multiple_of(idx * deep, deep), deep)

    def up_copy(idx):
        slot = lax.rem(idx, slots)
        return pltpu.make_async_copy(wu_ref.at[lines(idx), :], buf_ref.at[slot], sem.at[slot])

    lax.fori_loop(0, slots, lambda idx, _: up_copy(idx).start(), None)
    lax.fori_loop(0, own_ahead, lambda idx, _: own_copy(idx).start(), None)
    is_first = where_ref[0] == 0
    own = flat(own_ref)[:, :half]
    other = flat(other_ref)[:, :half]
    square = jnp.sum(own * own, axis=-1, keepdims=True)
    square = square + jnp.sum(other * other, axis=-1, keepdims=True)
    inv_rms = lax.rsqrt(square / (2 * half) + EPS)
    left = jnp.where(is_first, own, other)
    right = jnp.where(is_first, other, own)
    gain = gain_ref[...].astype(jnp.float32).reshape(1, -1)
    x_ref[:, :half] = (left * inv_rms * gain[:, :half]).astype(jnp.bfloat16)
    x_ref[:, half:] = (right * inv_rms * gain[:, half:]).astype(jnp.bfloat16)

    wide = math.gcd(out_ref.shape[1], 2048)

    def gate_step(idx, _):
        at = pl.ds(pl.multiple_of(idx * wide, wide), wide)
        gate = jnp.dot(x_ref[...], wg_ref[:, at], preferred_element_type=jnp.float32)
        gate_ref[:, at] = gate / (1.0 + jnp.exp(-gate))

    lax.fori_loop(0, out_ref.shape[1] // wide, gate_step, None)

    up_ref[...] = jnp.zeros_like(up_ref)

    def up_step(idx, _):
        up_copy(idx).wait()
        up_ref[...] += jnp.dot(
            x_ref[:, lines(idx)], buf_ref[lax.rem(idx, slots)], preferred_element_type=jnp.float32
        )

        @pl.when(idx + slots < chunks)
        def _():
            up_copy(idx + slots).start()

        @pl.when(idx + slots == chunks)
        def _():
            lax.fori_loop(own_ahead, own_chunks, lambda nth, _: own_copy(nth).start(), None)
            down.start()

    lax.fori_loop(0, chunks, up_step, None)
    out_ref[...] = (gate_ref[...] * up_ref[...]).astype(jnp.bfloat16)
    part_ref[...] = jnp.zeros_like(part_ref)

    def own_step(idx, _):
        own_copy(idx).wait()
        at = pl.ds(pl.multiple_of(idx * depth, depth), depth)
        part_ref[...] += jnp.dot(
            out_ref[:, at], own_buf_ref[idx], preferred_element_type=jnp.float32
        )

    lax.fori_loop(0, own_chunks, own_step, None)
    down.wait()


def down_other_kernel(
    where_ref, hid_ref, part_ref, extra_ref, held_ref, w_ref, out_ref, total_ref, buf_ref, sem
):
    held = held_ref.shape[0]
    start = (1 - where_ref[0]) * hid_ref.shape[1] + held
    rest = add_rows(hid_ref, held, w_ref, total_ref, buf_ref, sem, start)
    total_ref[...] = part_ref[...] + jnp.dot(
        hid_ref[:, :held], held_ref[...], preferred_element_type=jnp.float32
    )
    rest()
    total = total_ref[...]
    extra = flat(extra_ref)[:, -LANES:]
    lane = lax.broadcasted_iota(jnp.int32, extra.shape, 1)
    mine = (lane % EXPERTS == where_ref[1]) & (lane < 3 * EXPERTS)
    weight = jnp.sum(jnp.where(mine, extra, 0.0), axis=-1, keepdims=True)
    total = total * weight
    blocks, tok, _ = out_ref.shape
    for idx in range(blocks):
        out_ref[idx] = total[idx * tok : (idx + 1) * tok].astype(jnp.bfloat16)


def final_kernel(carried_ref, received_ref, out_ref):
    micro, dev, half = out_ref.shape
    moe = received_ref[0].astype(jnp.float32)
    for idx in range(1, received_ref.shape[0]):
        moe = moe + received_ref[idx].astype(jnp.float32)
    total = carried_ref[0, :, :half].astype(jnp.float32) + moe
    for idx in range(micro):
        out_ref[idx] = total[idx * dev : (idx + 1) * dev].astype(jnp.bfloat16)


SMEM = pl.BlockSpec(memory_space=pltpu.SMEM)
VMEM = pl.BlockSpec(memory_space=pltpu.VMEM)
ANY = pl.BlockSpec(memory_space=pl.ANY)


def call(kernel, out_shape, in_specs, args, scratch=(), limit=SMALL):
    return pl.pallas_call(
        kernel,
        out_shape=out_shape,
        in_specs=in_specs,
        out_specs=[VMEM] * len(out_shape) if isinstance(out_shape, tuple) else VMEM,
        scratch_shapes=scratch,
        compiler_params=pltpu.CompilerParams(vmem_limit_bytes=limit),
    )(*args)


def in_vmem(array):
    return pltpu.with_memory_space_constraint(array, pltpu.VMEM)


def in_hbm(array):
    return pltpu.with_memory_space_constraint(array, pltpu.HBM)


def swap(array, axis, mask):
    size = lax.axis_size(axis)
    return lax.ppermute(array, axis, [(i, i ^ mask) for i in range(size)])


def per_device(
    residual,
    queries,
    key_cache,
    value_cache,
    page_table,
    lengths,
    routes,
    gate_fixed,
    norm_gain,
    w_gate,
    w_up,
    w_down,
):
    micro_count, tok_dev, half = residual.shape
    side_size = lax.axis_size("side")
    tok = micro_count * tok_dev
    rows = tok * side_size
    span = side_size // EXPERTS
    small = SMALL + 64 * rows * half
    width = w_gate.shape[1]
    where = jnp.stack([lax.axis_index("tp"), lax.axis_index("side") // span]).astype(jnp.int32)
    small_args = (page_table, lengths, routes, gate_fixed)
    large_args = (residual, queries, key_cache, value_cache)
    local = call(
        attend_kernel,
        jax.ShapeDtypeStruct((side_size, tok, half + LANES), jnp.bfloat16),
        [SMEM] + [ANY] * 10,
        (where, *[in_hbm(arg) for arg in (*small_args, *large_args, w_gate, w_up)]),
        (
            *[pltpu.SMEM(arg.shape, arg.dtype) for arg in small_args],
            *[pltpu.VMEM(arg.shape, arg.dtype) for arg in large_args],
            pltpu.SemaphoreType.DMA((8,)),
        ),
        small,
    )
    gathered = lax.all_to_all(local, "side", split_axis=0, concat_axis=0, tiled=True)
    other = swap(gathered, "tp", 1)
    deep = math.gcd(2 * half, 256)
    slots = 6
    early = width * 1 // 2
    depth = math.gcd(width - early, early, 512)
    own_depth = math.gcd(width, 1024)
    held = pltpu.VMEM((early, half), w_down.dtype)

    def stream(count):
        return (
            pltpu.VMEM((count // depth, depth, half), w_down.dtype),
            pltpu.SemaphoreType.DMA((count // depth,)),
        )

    hidden, part, down_other = call(
        hidden_kernel,
        (
            pltpu.VMEM((rows, width), jnp.bfloat16),
            pltpu.VMEM((rows, half), jnp.float32),
            held,
        ),
        [SMEM] + [VMEM] * 4 + [ANY] * 2,
        (where, in_vmem(gathered), in_vmem(other), norm_gain, in_vmem(w_gate), in_hbm(w_up), in_hbm(w_down)),
        (
            pltpu.VMEM((rows, 2 * half), jnp.bfloat16),
            pltpu.VMEM((rows, width), jnp.float32),
            pltpu.VMEM((rows, width), jnp.float32),
            pltpu.VMEM((slots, deep, width), jnp.bfloat16),
            pltpu.VMEM((width // own_depth, own_depth, half), w_down.dtype),
            pltpu.SemaphoreType.DMA((slots,)),
            pltpu.SemaphoreType.DMA((width // own_depth,)),
            pltpu.SemaphoreType.DMA,
        ),
        SMALL + rows * half * 24 + slots * deep * width * 2 + rows * width * 4 + width * half * 2,
    )
    hidden_other = swap(hidden, "tp", 1)
    sent = call(
        down_other_kernel,
        jax.ShapeDtypeStruct((side_size, tok, half), jnp.bfloat16),
        [SMEM] + [VMEM] * 4 + [ANY],
        (where, hidden_other, in_vmem(part), gathered, in_vmem(down_other), in_hbm(w_down)),
        (pltpu.VMEM((rows, half), jnp.float32), *stream(width - early)),
        small + width * half * 2,
    )
    received = lax.all_to_all(sent, "side", split_axis=0, concat_axis=0, tiled=True)
    return call(
        final_kernel,
        jax.ShapeDtypeStruct(residual.shape, residual.dtype),
        [VMEM] * 2,
        (local, received),
        limit=small,
    )


def solution(mesh):
    in_specs = (
        P(None, ("groups", "side"), "tp"),
        P(None, ("groups", "side"), "tp"),
        P(("groups", "side"), None, "tp"),
        P(("groups", "side"), None, "tp"),
        P(None, ("groups", "side"), None),
        P(None, ("groups", "side")),
        P(None, ("groups", "side"), None),
        P(None, ("groups", "side")),
        P(),
        P(None, ("side", "tp")),
        P(None, ("side", "tp")),
        P("side", "tp"),
    )
    out_specs = P(None, ("groups", "side"), "tp")
    return jax.shard_map(
        per_device, mesh=mesh, in_specs=in_specs, out_specs=out_specs, check_vma=False
    )
```
